32 devices in a mesh: gx: 4 (over y, core), gy: 4 (over z), lev: 2 (over x).
Axes of the slice: x: 2, y: 2, z: 4, core: 2. Of those that a mesh axis runs over, the one named last changes fastest.
Arguments:
- model_state: float32 [2, 8, 2048, 2048], P(None, 'lev', 'gy', 'gx'), as said below
- cutoff: int32 [2, 8], P(None, 'lev'), may hold values from 5 to 10, as said below
- relax_rate: float32 [2, 8], P(None, 'lev'), may hold values from 0.2 to 1
- owner_map: int32 [2, 2], P('lev'), may hold values from 0 to 15
- era_store: float32 [16, 2, 8, 882], P(('gx', 'gy'), None, 'lev'), may hold values from -0.36 to 0.36
Outputs:
- nudged: float32 [2, 8, 2048, 2048], P(None, 'lev', 'gy', 'gx')
The draws below stay inside these ranges and needn't reach their ends.
Inputs may be any that keep to these rules, and one draw needn't show every extreme that they name: `cutoff`: each draw holds both the smallest and the largest value somewhere. `model_state`: finite values of order one.
All inputs are finite; a program needn't handle non-finite values.
Results may differ from the reference program's by a relative error of at most 0.00007.
Values sent between devices are 32-bit elements; how exact they have to be, the bound alone decides.
No kernel may reach another device: no remote copies, remote signals or barrier semaphores. Data moves between devices by JAX's collectives and lax.ppermute only.
A program may use at most 64 MiB of HBM per device.

```python
import math
import jax
import jax.numpy as jnp
from jax import lax

NX = 2048
NY = 2048
NVAR = 2
KC = 10
LEV_DEV = 4
NK = 21
LEVELS = 8
N_GX = 4
N_GY = 4
N_LEV = 2


def draw_model_state(key, part):
    subkeys = jax.random.split(key, 6)
    y_pos = jnp.arange(NY, dtype=jnp.int32)[:, None]
    x_pos = jnp.arange(NX, dtype=jnp.int32)[None, :]
    rough = jax.random.normal(subkeys[0], (NVAR, LEVELS, NY, NX), jnp.float32)
    amp_lo, amp_hi = (0.15, 0.45)
    factor = jax.random.uniform(subkeys[1], (NVAR, LEVELS, NY, NX), jnp.float32, 0.5, 1.5)
    total = rough * factor
    wave_x = jax.random.randint(subkeys[2], (6, NVAR, LEVELS, 1, 1), -KC, KC + 1)
    wave_y = jax.random.randint(subkeys[3], (6, NVAR, LEVELS, 1, 1), -KC, KC + 1)
    phases = jax.random.uniform(subkeys[4], (6, NVAR, LEVELS, 1, 1), jnp.float32, 0.0, 6.2831855)
    amplitude = jax.random.uniform(subkeys[5], (6, NVAR, LEVELS, 1, 1), jnp.float32, amp_lo, amp_hi)
    for wave_num in range(6):
        angle_x = jnp.mod(wave_x[wave_num] * x_pos, NX).astype(jnp.float32) * (6.2831855 / NX)
        angle_y = jnp.mod(wave_y[wave_num] * y_pos, NY).astype(jnp.float32) * (6.2831855 / NY)
        total = total + amplitude[wave_num] * jnp.cos(angle_x + angle_y + phases[wave_num])
    return total.astype(jnp.float32)


def draw_cutoff(key, part):
    count = NVAR * LEVELS
    values = jax.random.randint(key, (count,), KC // 2, KC + 1)
    first = jax.random.randint(jax.random.fold_in(key, 1), (), 0, count)
    other = jnp.mod(first + 1 + jax.random.randint(jax.random.fold_in(key, 2), (), 0, count - 1), count)
    values = values.at[first].set(KC)
    values = values.at[other].set(KC // 2)
    return values.reshape(NVAR, LEVELS).astype(jnp.int32)


def with_ends(drawn, stream_key, smallest, top_value):
    index_at = [jax.random.randint(jax.random.fold_in(stream_key, axis), (), 0, length) for axis, length in enumerate(drawn.shape)]
    main_axis = drawn.shape.index(max(drawn.shape))
    neighbour = index_at[:main_axis] + [(index_at[main_axis] + 1) % drawn.shape[main_axis]] + index_at[main_axis + 1:]
    return drawn.at[tuple(index_at)].set(smallest).at[tuple(neighbour)].set(top_value)


def steps_of(own_key, extent, pieces, least, largest):
    factor_of = 1.0
    for dim, blocks in pieces:
        heights = jax.random.uniform(jax.random.fold_in(jax.random.fold_in(own_key, 6), dim), (blocks,), jnp.float32, least / len(pieces), largest / len(pieces))
        factor_of = factor_of * jnp.repeat(jnp.exp(heights), extent[dim] // blocks).reshape((-1,) + (1,) * (len(extent) - 1 - dim))
    return factor_of


def scatter_about(rng, extent, width, reach, cuts=(), kind=jnp.bfloat16):
    entries = width * jax.random.normal(rng, extent, jnp.float32)
    if cuts:
        entries = entries * steps_of(rng, extent, cuts, -0.22, 0.18)
    return jnp.clip(entries, -reach, reach).astype(kind)


def setup_inputs(seed: int = 0) -> dict:
    streams_of = jax.random.split(jax.random.key(seed), 6)
    return {
        "model_state": draw_model_state(jax.random.fold_in(streams_of[5], 71), 0),
        "cutoff": draw_cutoff(jax.random.fold_in(streams_of[5], 71), 0),
        "relax_rate": jnp.clip(jnp.exp(math.log(1.0) - 1.609438 * jax.random.uniform(streams_of[2], (NVAR, LEVELS), jnp.float32) ** steps_of(streams_of[2], (NVAR, LEVELS), ((1, 2),), -0.2, 0.2)), 0.2, 1.0),
        "owner_map": with_ends(jax.random.randint(streams_of[3], (N_LEV, NVAR), 0, N_GX * N_GY), jax.random.fold_in(streams_of[3], 1), 0, (N_GX * N_GY) - 1).astype(jnp.int32),
        "era_store": scatter_about(streams_of[4], (N_GX * N_GY, NVAR, LEVELS, 2 * NK * NK), 0.06, 0.36, ((0, 16), (2, 2)), jnp.float32),
    }


def reference(model_state, cutoff, relax_rate, owner_map, era_store):
    wave_index = jnp.arange(NK, dtype=jnp.int32) - KC
    rows_y = jnp.mod(wave_index, NY)
    cols_x = jnp.mod(wave_index, NX)
    fields = model_state.reshape(NVAR * LEVELS, NY, NX)

    def forward(field):
        full = jnp.fft.fft2(field)
        picked = full[rows_y][:, cols_x] / (NX * NY)
        return jnp.stack([jnp.real(picked), jnp.imag(picked)])

    spectrum = lax.map(forward, fields).reshape(NVAR, LEVELS, 2, NK, NK)
    level_ids = jnp.arange(LEVELS, dtype=jnp.int32)
    owners = owner_map[level_ids // LEV_DEV]
    rows_var = []
    for var_num in range(NVAR):
        rows_var.append(era_store[owners[:, var_num], var_num, level_ids, :])
    analysis = jnp.stack(rows_var).reshape(NVAR, LEVELS, 2, NK, NK)
    total_sq = wave_index[:, None] ** 2 + wave_index[None, :] ** 2
    keep = (total_sq[None, None] <= (cutoff ** 2)[:, :, None, None]).astype(jnp.float32)
    increment = relax_rate[:, :, None, None, None] * keep[:, :, None] * (analysis - spectrum)
    flat_inc = increment.reshape(NVAR * LEVELS, 2, NK, NK)

    def inverse(delta):
        placed = jnp.zeros((NY, NX), dtype=jnp.complex64)
        placed = placed.at[rows_y[:, None], cols_x[None, :]].set(delta[0] + 1j * delta[1])
        return jnp.real(jnp.fft.ifft2(placed)) * (NX * NY)

    added = lax.map(inverse, flat_inc).reshape(NVAR, LEVELS, NY, NX)
    return model_state + added.astype(model_state.dtype)
```

```python
import functools

import jax
import jax.numpy as jnp
import ml_dtypes
import numpy as np
from jax import lax
from jax.experimental import pallas as pl
from jax.experimental.pallas import tpu as pltpu
from jax.sharding import PartitionSpec as P

NX = 2048
NY = 2048
KC = 10
NK = 21
F = 8
GROUP = 32
SLOTS = 24
PACKED = SLOTS * GROUP


def basis(positions, length):
    wave = np.concatenate([np.arange(KC + 1), np.arange(1, KC + 1)])
    angle = np.mod(positions[:, None] * wave[None, :], length) * (2 * np.pi / length)
    return np.where(np.arange(NK) <= KC, np.cos(angle), np.sin(angle))


def halves(table):
    high = table.astype(ml_dtypes.bfloat16)
    low = (table - high.astype(np.float64)).astype(ml_dtypes.bfloat16)
    return high, low


def forward_tables(n_gx, n_gy):
    weight = np.where(np.arange(NK) == 0, 1.0, 2.0)
    high, low = halves(basis(np.arange(NY), NY) * weight / NY)
    ny = NY // n_gy
    along_y = np.zeros((n_gy, 64, ny), ml_dtypes.bfloat16)
    along_y[:, :NK] = high.reshape(n_gy, ny, NK).transpose(0, 2, 1)
    along_y[:, 32 : 32 + NK] = low.reshape(n_gy, ny, NK).transpose(0, 2, 1)
    high, low = halves(basis(np.arange(NX), NX) * weight / NX)
    nx = NX // n_gx
    along_x = np.zeros((n_gx, nx, 256), ml_dtypes.bfloat16)
    for group in range(4):
        at = group * GROUP
        along_x[:, :, at : at + NK] = high.reshape(n_gx, nx, NK)
        along_x[:, :, 128 + at : 128 + at + NK] = low.reshape(n_gx, nx, NK)
    return along_y, along_x


def inverse_tables(n_gx, n_gy):
    high, low = halves(basis(np.arange(NY), NY))
    ny = NY // n_gy
    along_y = np.zeros((n_gy, ny, 128), ml_dtypes.bfloat16)
    for slot in range(NK):
        at = (slot % 4) * (SLOTS // 4) + slot // 4
        along_y[:, :, at] = high[:, slot].reshape(n_gy, ny)
        along_y[:, :, SLOTS + at] = low[:, slot].reshape(n_gy, ny)
        along_y[:, :, 2 * SLOTS + at] = high[:, slot].reshape(n_gy, ny)
    high, low = halves(basis(np.arange(NX), NX))
    nx = NX // n_gx
    along_x = np.zeros((n_gx, 256, nx), ml_dtypes.bfloat16)
    for group in range(4):
        at = group * GROUP
        along_x[:, at : at + NK] = high.reshape(n_gx, nx, NK).transpose(0, 2, 1)
        along_x[:, 128 + at : 128 + at + NK] = low.reshape(n_gx, nx, NK).transpose(0, 2, 1)
    return along_y, along_x


def split(value):
    high = value.astype(jnp.bfloat16)
    return high, (value - high.astype(jnp.float32)).astype(jnp.bfloat16)


def dot(left, right):
    return jnp.dot(left, right, preferred_element_type=jnp.float32)


def lane_group(shape):
    return lax.broadcasted_iota(jnp.int32, shape, 1) // GROUP


def analysis_rows(store):
    pieces = []
    for row in range(2 * NK):
        at = row * NK
        base = at // 128 * 128
        off = at - base
        width = 128 if off + NK <= 128 else 256
        window = store[:, base : base + width]
        pieces.append(pltpu.roll(window, (width - off) % width, 1)[:, :128] if off else window[:, :128])
    high, low = split(jnp.concatenate(pieces, axis=0))
    wave = lax.broadcasted_iota(jnp.int32, (128, 128), 0) - KC
    column = lax.broadcasted_iota(jnp.int32, (128, 128), 1) % GROUP
    number = jnp.where(column <= KC, column, column - KC)
    plus = jnp.where(wave == number, 1.0, 0.0)
    minus = jnp.where((wave == -number) & (number > 0), 1.0, 0.0)
    fold = jnp.where(column <= KC, plus + minus, plus - minus)
    fold = jnp.where(column < NK, fold, 0.0).astype(jnp.bfloat16)
    folded = dot(high, fold) + dot(low, fold)
    part = [folded[8 * row : 8 * row + 8] for row in range(2 * NK)]
    real, imag = part[:NK], part[NK:]
    even = lax.broadcasted_iota(jnp.int32, (8, 128), 1) % GROUP <= KC
    rows = [jnp.where(even, real[KC], -imag[KC])]
    for wave in range(1, KC + 1):
        up, down = KC + wave, KC - wave
        rows.append(jnp.where(even, real[up] + real[down], -(imag[up] + imag[down])))
    for wave in range(1, KC + 1):
        up, down = KC + wave, KC - wave
        rows.append(-jnp.where(even, imag[up] - imag[down], real[up] - real[down]))
    return rows


def pack(rows):
    group = lane_group((8, 128))
    blocks = []
    for block in range(SLOTS // 4):
        total = jnp.zeros((8, 128), jnp.float32)
        for j in range(4):
            if 4 * block + j < len(rows):
                total = jnp.where(group == j, rows[4 * block + j], total)
        blocks.append(total)
    return jnp.concatenate(blocks, axis=1)


def per_field(values):
    row = lax.broadcasted_iota(jnp.int32, (F, 1), 0)
    total = jnp.full((F, 1), values[0])
    for field in range(1, F):
        total = jnp.where(row == field, values[field], total)
    return total


def project_kernel(
    n_gy, levels, owner, cutoff, relax, era, field_hbm, fy_hbm, fx_hbm, iy_hbm, ix_hbm,
    share, field, iy, ix, store, fy, fx, bands, field_sem, table_sem,
):
    gx, gy = lax.axis_index("gx"), lax.axis_index("gy")
    tables = [
        pltpu.make_async_copy(src, dst, table_sem.at[n])
        for n, (src, dst) in enumerate(
            ((fy_hbm.at[gy], fy), (fx_hbm.at[gx], fx), (iy_hbm.at[gy], iy), (ix_hbm.at[gx], ix))
        )
    ]
    tables[0].start()
    for f in range(F):
        pltpu.make_async_copy(field_hbm.at[f // levels, f % levels], field.at[f], field_sem.at[f]).start()
    for copy in tables[1:]:
        copy.start()

    store[...] = jnp.zeros_like(store)
    for var in range(F // levels):
        store[var * levels : (var + 1) * levels, : 2 * NK * NK] = era[0, var]
    analysis = pack(analysis_rows(store[...]))
    me = gx * n_gy + gy
    mine = per_field([(owner[0, f // levels] == me).astype(jnp.int32) for f in range(F)])
    limit = per_field([cutoff[f // levels, f % levels] for f in range(F)])
    rate = per_field([relax[f // levels, f % levels] for f in range(F)])
    lane = lax.broadcasted_iota(jnp.int32, (F, PACKED), 1)
    slot, column = lane // GROUP, lane % GROUP
    ky = jnp.where(slot <= KC, slot, slot - KC)
    kx = jnp.where(column <= KC, column, column - KC)
    factor = jnp.where(ky * ky + kx * kx <= limit * limit, rate, 0.0)
    analysis = jnp.where(mine == 1, analysis, 0.0)

    tables[0].wait()

    def one(f, _):
        pltpu.make_async_copy(field_hbm.at[0, 0], field.at[f], field_sem.at[f]).wait()
        high, low = split(field[f])
        wide = dot(fy[...], high)
        band = wide[:SLOTS] + wide[32 : 32 + SLOTS] + dot(fy[:32], low)[:SLOTS]
        for tile in range(bands.shape[0]):
            bands[tile, pl.ds(f, SLOTS, stride=F), :] = band[:, 128 * tile : 128 * tile + 128]
        return 0

    lax.fori_loop(0, F, one, 0)
    tables[1].wait()
    high, low = split(jnp.concatenate([bands[tile] for tile in range(bands.shape[0])], axis=1))
    both = dot(high, fx[...])
    spectrum = both[:, :128] + both[:, 128:] + dot(low, fx[:, :128])
    spectrum = pack([spectrum[F * slot : F * slot + F] for slot in range(SLOTS)])
    share[...] = factor * (analysis - spectrum)
    tables[2].wait()
    tables[3].wait()


def nudge_kernel(levels, chunk, mine, other, field, iy, ix, out_hbm, out, bands, sem):
    total = mine[...] + other[...]
    group = lane_group((F, 128))
    rows = []
    for j in range(4):
        for block in range(SLOTS // 4):
            rows.append(jnp.where(group == j, total[:, 128 * block : 128 * block + 128], 0.0))
    high, low = split(jnp.concatenate(rows, axis=0))
    wide = dot(high, ix[:128]) + dot(high, ix[128:]) + dot(low, ix[:128])
    for tile in range(bands.shape[0]):
        bands[tile] = wide[:, 128 * tile : 128 * tile + 128]
    ny, nx = out.shape[1:]
    steps = ny // chunk

    def one(f, _):
        band = [bands[tile, pl.ds(f, SLOTS, stride=F), :] for tile in range(bands.shape[0])]
        band = jnp.concatenate(band, axis=1)
        high = band.astype(jnp.bfloat16).astype(jnp.float32)
        stacked = jnp.concatenate([high, high, band - high, jnp.zeros((128 - 3 * SLOTS, nx), jnp.float32)], axis=0)
        stacked = stacked.astype(jnp.bfloat16)
        for step in range(steps):
            at = pl.ds(step * chunk, chunk)
            out[f, at] = field[f, at] + dot(iy[at], stacked)
            pltpu.make_async_copy(
                out.at[f, at], out_hbm.at[f // levels, f % levels, at], sem.at[f * steps + step]
            ).start()
        return 0

    lax.fori_loop(0, F, one, 0)

    def end(n, _):
        f, step = n // steps, n % steps
        at = pl.ds(pl.multiple_of(step * chunk, chunk), chunk)
        pltpu.make_async_copy(out.at[f, at], out_hbm.at[f // levels, f % levels, at], sem.at[n]).wait()
        return 0

    lax.fori_loop(0, F * steps, end, 0)


def swap(value, axis, size, bit):
    return lax.ppermute(value, axis, [(i, i ^ bit) for i in range(size)])


def body(n_gx, n_gy, model_state, cutoff, relax_rate, owner_map, era_store):
    nvar, levels, ny, nx = model_state.shape
    fy, fx = forward_tables(n_gx, n_gy)
    iy, ix = inverse_tables(n_gx, n_gy)
    smem = pl.BlockSpec(memory_space=pltpu.SMEM)
    vmem = pl.BlockSpec(memory_space=pltpu.VMEM)
    hbm = pl.BlockSpec(memory_space=pl.ANY)
    share, field, iy, ix = pl.pallas_call(
        functools.partial(project_kernel, n_gy, levels),
        out_shape=(
            pltpu.VMEM((F, PACKED), jnp.float32),
            pltpu.VMEM((F, ny, nx), jnp.float32),
            pltpu.VMEM((ny, 128), jnp.bfloat16),
            pltpu.VMEM((256, nx), jnp.bfloat16),
        ),
        in_specs=[smem, smem, smem, vmem, hbm, hbm, hbm, hbm, hbm],
        out_specs=[vmem] * 4,
        scratch_shapes=[
            pltpu.VMEM((F, 1024), jnp.float32),
            pltpu.VMEM((64, ny), jnp.bfloat16),
            pltpu.VMEM((nx, 256), jnp.bfloat16),
            pltpu.VMEM((nx // 128, SLOTS * F, 128), jnp.float32),
            pltpu.SemaphoreType.DMA((F,)),
            pltpu.SemaphoreType.DMA((4,)),
        ],
        compiler_params=pltpu.CompilerParams(vmem_limit_bytes=20 * 2**20),
        name="project",
    )(owner_map, cutoff, relax_rate, era_store, model_state, fy, fx, iy, ix)

    steps = [("gx", n_gx, 1 << bit) for bit in range(n_gx.bit_length() - 1)]
    steps += [("gy", n_gy, 1 << bit) for bit in range(n_gy.bit_length() - 1)]
    for step in steps[:-1]:
        share = share + swap(share, *step)
    other = swap(share, *steps[-1])

    chunk = min(ny, 256)
    nudged = pl.pallas_call(
        functools.partial(nudge_kernel, levels, chunk),
        out_shape=jax.ShapeDtypeStruct(model_state.shape, jnp.float32),
        in_specs=[vmem] * 5,
        out_specs=hbm,
        scratch_shapes=[
            pltpu.VMEM((F, ny, nx), jnp.float32),
            pltpu.VMEM((nx // 128, SLOTS * F, 128), jnp.float32),
            pltpu.SemaphoreType.DMA((F * (ny // chunk),)),
        ],
        compiler_params=pltpu.CompilerParams(vmem_limit_bytes=30 * 2**20),
        name="nudge",
    )(share, other, field, iy, ix)
    return nudged


def solution(mesh):
    n_gx, n_gy = mesh.shape["gx"], mesh.shape["gy"]
    placed = (
        P(None, "lev", "gy", "gx"),
        P(None, "lev"),
        P(None, "lev"),
        P("lev", None),
        P(("gx", "gy"), None, "lev", None),
    )
    return jax.shard_map(
        functools.partial(body, n_gx, n_gy),
        mesh=mesh,
        in_specs=placed,
        out_specs=P(None, "lev", "gy", "gx"),
        check_vma=False,
    )
```

```python
import functools

import jax
import jax.numpy as jnp
import ml_dtypes
import numpy as np
from jax import lax
from jax.experimental import pallas as pl
from jax.experimental.pallas import tpu as pltpu
from jax.sharding import PartitionSpec as P

NX = 2048
NY = 2048
KC = 10
NK = 21
F = 8
GROUP = 32
SLOTS = 24
PACKED = SLOTS * GROUP


def basis(positions, length):
    wave = np.concatenate([np.arange(KC + 1), np.arange(1, KC + 1)])
    angle = np.mod(positions[:, None] * wave[None, :], length) * (2 * np.pi / length)
    return np.where(np.arange(NK) <= KC, np.cos(angle), np.sin(angle))


def halves(table):
    high = table.astype(ml_dtypes.bfloat16)
    low = (table - high.astype(np.float64)).astype(ml_dtypes.bfloat16)
    return high, low


def forward_tables(n_gx, n_gy):
    weight = np.where(np.arange(NK) == 0, 1.0, 2.0)
    high, low = halves(basis(np.arange(NY), NY) * weight / NY)
    ny = NY // n_gy
    along_y = np.zeros((n_gy, 64, ny), ml_dtypes.bfloat16)
    along_y[:, :NK] = high.reshape(n_gy, ny, NK).transpose(0, 2, 1)
    along_y[:, 32 : 32 + NK] = low.reshape(n_gy, ny, NK).transpose(0, 2, 1)
    high, low = halves(basis(np.arange(NX), NX) * weight / NX)
    nx = NX // n_gx
    along_x = np.zeros((n_gx, nx, 256), ml_dtypes.bfloat16)
    for group in range(4):
        at = group * GROUP
        along_x[:, :, at : at + NK] = high.reshape(n_gx, nx, NK)
        along_x[:, :, 128 + at : 128 + at + NK] = low.reshape(n_gx, nx, NK)
    return along_y, along_x


def inverse_tables(n_gx, n_gy):
    high, low = halves(basis(np.arange(NY), NY))
    ny = NY // n_gy
    along_y = np.zeros((n_gy, ny, 128), ml_dtypes.bfloat16)
    for slot in range(NK):
        at = (slot % 4) * (SLOTS // 4) + slot // 4
        along_y[:, :, at] = high[:, slot].reshape(n_gy, ny)
        along_y[:, :, SLOTS + at] = low[:, slot].reshape(n_gy, ny)
        along_y[:, :, 2 * SLOTS + at] = high[:, slot].reshape(n_gy, ny)
    high, low = halves(basis(np.arange(NX), NX))
    nx = NX // n_gx
    along_x = np.zeros((n_gx, 256, nx), ml_dtypes.bfloat16)
    for group in range(4):
        at = group * GROUP
        along_x[:, at : at + NK] = high.reshape(n_gx, nx, NK).transpose(0, 2, 1)
        along_x[:, 128 + at : 128 + at + NK] = low.reshape(n_gx, nx, NK).transpose(0, 2, 1)
    return along_y, along_x


def split(value):
    high = value.astype(jnp.bfloat16)
    return high, (value - high.astype(jnp.float32)).astype(jnp.bfloat16)


def dot(left, right):
    return jnp.dot(left, right, preferred_element_type=jnp.float32)


def lane_group(shape):
    return lax.broadcasted_iota(jnp.int32, shape, 1) // GROUP


def analysis_rows(store):
    pieces = []
    for row in range(2 * NK):
        at = row * NK
        base = at // 128 * 128
        off = at - base
        width = 128 if off + NK <= 128 else 256
        window = store[:, base : base + width]
        pieces.append(pltpu.roll(window, (width - off) % width, 1)[:, :128] if off else window[:, :128])
    high, low = split(jnp.concatenate(pieces, axis=0))
    wave = lax.broadcasted_iota(jnp.int32, (128, 128), 0) - KC
    column = lax.broadcasted_iota(jnp.int32, (128, 128), 1) % GROUP
    number = jnp.where(column <= KC, column, column - KC)
    plus = jnp.where(wave == number, 1.0, 0.0)
    minus = jnp.where((wave == -number) & (number > 0), 1.0, 0.0)
    fold = jnp.where(column <= KC, plus + minus, plus - minus)
    fold = jnp.where(column < NK, fold, 0.0).astype(jnp.bfloat16)
    folded = dot(high, fold) + dot(low, fold)
    part = [folded[8 * row : 8 * row + 8] for row in range(2 * NK)]
    real, imag = part[:NK], part[NK:]
    even = lax.broadcasted_iota(jnp.int32, (8, 128), 1) % GROUP <= KC
    rows = [jnp.where(even, real[KC], -imag[KC])]
    for wave in range(1, KC + 1):
        up, down = KC + wave, KC - wave
        rows.append(jnp.where(even, real[up] + real[down], -(imag[up] + imag[down])))
    for wave in range(1, KC + 1):
        up, down = KC + wave, KC - wave
        rows.append(-jnp.where(even, imag[up] - imag[down], real[up] - real[down]))
    return rows


def pack(rows):
    group = lane_group((8, 128))
    blocks = []
    for block in range(SLOTS // 4):
        total = jnp.zeros((8, 128), jnp.float32)
        for j in range(4):
            if 4 * block + j < len(rows):
                total = jnp.where(group == j, rows[4 * block + j], total)
        blocks.append(total)
    return jnp.concatenate(blocks, axis=1)


def per_field(values):
    row = lax.broadcasted_iota(jnp.int32, (F, 1), 0)
    total = jnp.full((F, 1), values[0])
    for field in range(1, F):
        total = jnp.where(row == field, values[field], total)
    return total


def project_kernel(
    n_gy, levels, owner_hbm, cutoff_hbm, relax_hbm, era_hbm, field_hbm, fy_hbm, fx_hbm, iy_hbm, ix_hbm,
    share, field, iy, ix, owner, cutoff, relax, era, store, fy, fx, bands, field_sem, small_sem, table_sem,
):
    gx, gy = lax.axis_index("gx"), lax.axis_index("gy")
    tables = [
        pltpu.make_async_copy(src, dst, table_sem.at[n])
        for n, (src, dst) in enumerate(
            ((fy_hbm.at[gy], fy), (fx_hbm.at[gx], fx), (iy_hbm.at[gy], iy), (ix_hbm.at[gx], ix))
        )
    ]
    small = [
        pltpu.make_async_copy(src, dst, small_sem.at[n])
        for n, (src, dst) in enumerate(
            ((era_hbm, era), (owner_hbm, owner), (cutoff_hbm, cutoff), (relax_hbm, relax))
        )
    ]
    for copy in small:
        copy.start()
    tables[0].start()
    for f in range(F):
        pltpu.make_async_copy(field_hbm.at[f // levels, f % levels], field.at[f], field_sem.at[f]).start()
    for copy in tables[1:]:
        copy.start()

    store[...] = jnp.zeros_like(store)
    for copy in small:
        copy.wait()
    for var in range(F // levels):
        store[var * levels : (var + 1) * levels, : 2 * NK * NK] = era[0, var]
    analysis = pack(analysis_rows(store[...]))
    me = gx * n_gy + gy
    mine = per_field([(owner[0, f // levels] == me).astype(jnp.int32) for f in range(F)])
    limit = per_field([cutoff[f // levels, f % levels] for f in range(F)])
    rate = per_field([relax[f // levels, f % levels] for f in range(F)])
    lane = lax.broadcasted_iota(jnp.int32, (F, PACKED), 1)
    slot, column = lane // GROUP, lane % GROUP
    ky = jnp.where(slot <= KC, slot, slot - KC)
    kx = jnp.where(column <= KC, column, column - KC)
    factor = jnp.where(ky * ky + kx * kx <= limit * limit, rate, 0.0)
    analysis = jnp.where(mine == 1, analysis, 0.0)

    tables[0].wait()

    def one(f, _):
        pltpu.make_async_copy(field_hbm.at[0, 0], field.at[f], field_sem.at[f]).wait()
        high, low = split(field[f])
        wide = dot(fy[...], high)
        band = wide[:SLOTS] + wide[32 : 32 + SLOTS] + dot(fy[:32], low)[:SLOTS]
        for tile in range(bands.shape[0]):
            bands[tile, pl.ds(f, SLOTS, stride=F), :] = band[:, 128 * tile : 128 * tile + 128]
        return 0

    lax.fori_loop(0, F, one, 0)
    tables[1].wait()
    high, low = split(jnp.concatenate([bands[tile] for tile in range(bands.shape[0])], axis=1))
    both = dot(high, fx[...])
    spectrum = both[:, :128] + both[:, 128:] + dot(low, fx[:, :128])
    spectrum = pack([spectrum[F * slot : F * slot + F] for slot in range(SLOTS)])
    share[...] = factor * (analysis - spectrum)
    tables[2].wait()
    tables[3].wait()


def nudge_kernel(levels, chunk, mine, other, field, iy, ix, out_hbm, out, bands, sem):
    total = mine[...] + other[...]
    group = lane_group((F, 128))
    rows = []
    for j in range(4):
        for block in range(SLOTS // 4):
            rows.append(jnp.where(group == j, total[:, 128 * block : 128 * block + 128], 0.0))
    high, low = split(jnp.concatenate(rows, axis=0))
    wide = dot(high, ix[:128]) + dot(high, ix[128:]) + dot(low, ix[:128])
    for tile in range(bands.shape[0]):
        bands[tile] = wide[:, 128 * tile : 128 * tile + 128]
    ny, nx = out.shape[1:]
    steps = ny // chunk

    def one(f, _):
        band = [bands[tile, pl.ds(f, SLOTS, stride=F), :] for tile in range(bands.shape[0])]
        band = jnp.concatenate(band, axis=1)
        high = band.astype(jnp.bfloat16).astype(jnp.float32)
        stacked = jnp.concatenate([high, high, band - high, jnp.zeros((128 - 3 * SLOTS, nx), jnp.float32)], axis=0)
        stacked = stacked.astype(jnp.bfloat16)
        for step in range(steps):
            at = pl.ds(step * chunk, chunk)
            out[f, at] = field[f, at] + dot(iy[at], stacked)
            pltpu.make_async_copy(
                out.at[f, at], out_hbm.at[f // levels, f % levels, at], sem.at[f * steps + step]
            ).start()
        return 0

    lax.fori_loop(0, F, one, 0)

    def end(n, _):
        f, step = n // steps, n % steps
        at = pl.ds(pl.multiple_of(step * chunk, chunk), chunk)
        pltpu.make_async_copy(out.at[f, at], out_hbm.at[f // levels, f % levels, at], sem.at[n]).wait()
        return 0

    lax.fori_loop(0, F * steps, end, 0)


def in_hbm(value):
    return pltpu.with_memory_space_constraint(jnp.asarray(value), pltpu.HBM)


def swap(value, axis, size, bit):
    return lax.ppermute(value, axis, [(i, i ^ bit) for i in range(size)])


def body(n_gx, n_gy, model_state, cutoff, relax_rate, owner_map, era_store):
    nvar, levels, ny, nx = model_state.shape
    fy, fx = forward_tables(n_gx, n_gy)
    iy, ix = inverse_tables(n_gx, n_gy)
    vmem = pl.BlockSpec(memory_space=pltpu.VMEM)
    hbm = pl.BlockSpec(memory_space=pltpu.HBM)
    share, field, iy, ix = pl.pallas_call(
        functools.partial(project_kernel, n_gy, levels),
        out_shape=(
            pltpu.VMEM((F, PACKED), jnp.float32),
            pltpu.VMEM((F, ny, nx), jnp.float32),
            pltpu.VMEM((ny, 128), jnp.bfloat16),
            pltpu.VMEM((256, nx), jnp.bfloat16),
        ),
        in_specs=[hbm] * 9,
        out_specs=[vmem] * 4,
        scratch_shapes=[
            pltpu.SMEM(owner_map.shape, jnp.int32),
            pltpu.SMEM(cutoff.shape, jnp.int32),
            pltpu.SMEM(relax_rate.shape, jnp.float32),
            pltpu.VMEM(era_store.shape, jnp.float32),
            pltpu.VMEM((F, 1024), jnp.float32),
            pltpu.VMEM((64, ny), jnp.bfloat16),
            pltpu.VMEM((nx, 256), jnp.bfloat16),
            pltpu.VMEM((nx // 128, SLOTS * F, 128), jnp.float32),
            pltpu.SemaphoreType.DMA((F,)),
            pltpu.SemaphoreType.DMA((4,)),
            pltpu.SemaphoreType.DMA((4,)),
        ],
        compiler_params=pltpu.CompilerParams(vmem_limit_bytes=20 * 2**20),
        name="project",
    )(*(in_hbm(value) for value in (owner_map, cutoff, relax_rate, era_store, model_state, fy, fx, iy, ix)))

    steps = [("gx", n_gx, 1 << bit) for bit in range(n_gx.bit_length() - 1)]
    steps += [("gy", n_gy, 1 << bit) for bit in range(n_gy.bit_length() - 1)]
    for step in steps[:-1]:
        share = share + swap(share, *step)
    other = swap(share, *steps[-1])

    chunk = min(ny, 256)
    nudged = pl.pallas_call(
        functools.partial(nudge_kernel, levels, chunk),
        out_shape=jax.ShapeDtypeStruct(model_state.shape, jnp.float32),
        in_specs=[vmem] * 5,
        out_specs=hbm,
        scratch_shapes=[
            pltpu.VMEM((F, ny, nx), jnp.float32),
            pltpu.VMEM((nx // 128, SLOTS * F, 128), jnp.float32),
            pltpu.SemaphoreType.DMA((F * (ny // chunk),)),
        ],
        compiler_params=pltpu.CompilerParams(vmem_limit_bytes=30 * 2**20),
        name="nudge",
    )(share, other, field, iy, ix)
    return nudged


def solution(mesh):
    n_gx, n_gy = mesh.shape["gx"], mesh.shape["gy"]
    placed = (
        P(None, "lev", "gy", "gx"),
        P(None, "lev"),
        P(None, "lev"),
        P("lev", None),
        P(("gx", "gy"), None, "lev", None),
    )
    return jax.shard_map(
        functools.partial(body, n_gx, n_gy),
        mesh=mesh,
        in_specs=placed,
        out_specs=P(None, "lev", "gy", "gx"),
        check_vma=False,
    )
```

```python
import functools

import jax
import jax.numpy as jnp
import ml_dtypes
import numpy as np
from jax import lax
from jax.experimental import pallas as pl
from jax.experimental.pallas import tpu as pltpu
from jax.sharding import PartitionSpec as P

NX = 2048
NY = 2048
KC = 10
NK = 21
F = 8
GROUP = 32
SLOTS = 24
PACKED = SLOTS * GROUP


def basis(positions, length):
    wave = np.concatenate([np.arange(KC + 1), np.arange(1, KC + 1)])
    angle = np.mod(positions[:, None] * wave[None, :], length) * (2 * np.pi / length)
    return np.where(np.arange(NK) <= KC, np.cos(angle), np.sin(angle))


def halves(table):
    high = table.astype(ml_dtypes.bfloat16)
    low = (table - high.astype(np.float64)).astype(ml_dtypes.bfloat16)
    return high, low


def forward_tables(n_gx, n_gy):
    weight = np.where(np.arange(NK) == 0, 1.0, 2.0)
    high, low = halves(basis(np.arange(NY), NY) * weight / NY)
    ny = NY // n_gy
    along_y = np.zeros((n_gy, 64, ny), ml_dtypes.bfloat16)
    along_y[:, :NK] = high.reshape(n_gy, ny, NK).transpose(0, 2, 1)
    along_y[:, 32 : 32 + NK] = low.reshape(n_gy, ny, NK).transpose(0, 2, 1)
    high, low = halves(basis(np.arange(NX), NX) * weight / NX)
    nx = NX // n_gx
    along_x = np.zeros((n_gx, nx, 256), ml_dtypes.bfloat16)
    for group in range(4):
        at = group * GROUP
        along_x[:, :, at : at + NK] = high.reshape(n_gx, nx, NK)
        along_x[:, :, 128 + at : 128 + at + NK] = low.reshape(n_gx, nx, NK)
    return along_y, along_x


def inverse_tables(n_gx, n_gy):
    high, low = halves(basis(np.arange(NY), NY))
    ny = NY // n_gy
    along_y = np.zeros((n_gy, ny, 128), ml_dtypes.bfloat16)
    for slot in range(NK):
        at = (slot % 4) * (SLOTS // 4) + slot // 4
        along_y[:, :, at] = high[:, slot].reshape(n_gy, ny)
        along_y[:, :, SLOTS + at] = low[:, slot].reshape(n_gy, ny)
        along_y[:, :, 2 * SLOTS + at] = high[:, slot].reshape(n_gy, ny)
    high, low = halves(basis(np.arange(NX), NX))
    nx = NX // n_gx
    along_x = np.zeros((n_gx, 256, nx), ml_dtypes.bfloat16)
    for group in range(4):
        at = group * GROUP
        along_x[:, at : at + NK] = high.reshape(n_gx, nx, NK).transpose(0, 2, 1)
        along_x[:, 128 + at : 128 + at + NK] = low.reshape(n_gx, nx, NK).transpose(0, 2, 1)
    return along_y, along_x


def split(value):
    high = value.astype(jnp.bfloat16)
    return high, (value - high.astype(jnp.float32)).astype(jnp.bfloat16)


def dot(left, right):
    return jnp.dot(left, right, preferred_element_type=jnp.float32)


def lane_group(shape):
    return lax.broadcasted_iota(jnp.int32, shape, 1) // GROUP


def analysis_rows(store):
    pieces = []
    for row in range(2 * NK):
        at = row * NK
        base = at // 128 * 128
        off = at - base
        width = 128 if off + NK <= 128 else 256
        window = store[:, base : base + width]
        pieces.append(pltpu.roll(window, (width - off) % width, 1)[:, :128] if off else window[:, :128])
    high, low = split(jnp.concatenate(pieces, axis=0))
    wave = lax.broadcasted_iota(jnp.int32, (128, 128), 0) - KC
    column = lax.broadcasted_iota(jnp.int32, (128, 128), 1) % GROUP
    number = jnp.where(column <= KC, column, column - KC)
    plus = jnp.where(wave == number, 1.0, 0.0)
    minus = jnp.where((wave == -number) & (number > 0), 1.0, 0.0)
    fold = jnp.where(column <= KC, plus + minus, plus - minus)
    fold = jnp.where(column < NK, fold, 0.0).astype(jnp.bfloat16)
    folded = dot(high, fold) + dot(low, fold)
    part = [folded[8 * row : 8 * row + 8] for row in range(2 * NK)]
    real, imag = part[:NK], part[NK:]
    even = lax.broadcasted_iota(jnp.int32, (8, 128), 1) % GROUP <= KC
    rows = [jnp.where(even, real[KC], -imag[KC])]
    for wave in range(1, KC + 1):
        up, down = KC + wave, KC - wave
        rows.append(jnp.where(even, real[up] + real[down], -(imag[up] + imag[down])))
    for wave in range(1, KC + 1):
        up, down = KC + wave, KC - wave
        rows.append(-jnp.where(even, imag[up] - imag[down], real[up] - real[down]))
    return rows


def pack(rows):
    group = lane_group((8, 128))
    blocks = []
    for block in range(SLOTS // 4):
        total = jnp.zeros((8, 128), jnp.float32)
        for j in range(4):
            if 4 * block + j < len(rows):
                total = jnp.where(group == j, rows[4 * block + j], total)
        blocks.append(total)
    return jnp.concatenate(blocks, axis=1)


def per_field(values):
    row = lax.broadcasted_iota(jnp.int32, (F, 1), 0)
    total = jnp.full((F, 1), values[0])
    for field in range(1, F):
        total = jnp.where(row == field, values[field], total)
    return total


def project_kernel(
    n_gy, levels, owner_hbm, cutoff_hbm, relax_hbm, era_hbm, field_hbm, fy_hbm, fx_hbm, iy_hbm, ix_hbm,
    share, field, iy, ix, owner, cutoff, relax, era, store, fy, fx, bands, field_sem, small_sem, table_sem,
):
    gx, gy = lax.axis_index("gx"), lax.axis_index("gy")
    tables = [
        pltpu.make_async_copy(src, dst, table_sem.at[n])
        for n, (src, dst) in enumerate(
            ((fy_hbm.at[gy], fy), (fx_hbm.at[gx], fx), (iy_hbm.at[gy], iy), (ix_hbm.at[gx], ix))
        )
    ]
    small = [
        pltpu.make_async_copy(src, dst, small_sem.at[n])
        for n, (src, dst) in enumerate(
            ((era_hbm, era), (owner_hbm, owner), (cutoff_hbm, cutoff), (relax_hbm, relax))
        )
    ]
    for copy in small:
        copy.start()
    tables[0].start()
    window = 4
    for f, pieces in enumerate((1, 1, 1, 1)):
        rows = field.shape[1] // pieces
        for piece in range(pieces):
            at = pl.ds(piece * rows, rows)
            pltpu.make_async_copy(field_hbm.at[f // levels, f % levels, at], field.at[f, at], field_sem.at[f]).start()
    for copy in tables[1:]:
        copy.start()

    store[...] = jnp.zeros_like(store)
    for copy in small:
        copy.wait()
    for var in range(F // levels):
        store[var * levels : (var + 1) * levels, : 2 * NK * NK] = era[0, var]
    analysis = pack(analysis_rows(store[...]))
    me = gx * n_gy + gy
    mine = per_field([(owner[0, f // levels] == me).astype(jnp.int32) for f in range(F)])
    limit = per_field([cutoff[f // levels, f % levels] for f in range(F)])
    rate = per_field([relax[f // levels, f % levels] for f in range(F)])
    lane = lax.broadcasted_iota(jnp.int32, (F, PACKED), 1)
    slot, column = lane // GROUP, lane % GROUP
    ky = jnp.where(slot <= KC, slot, slot - KC)
    kx = jnp.where(column <= KC, column, column - KC)
    factor = jnp.where(ky * ky + kx * kx <= limit * limit, rate, 0.0)
    analysis = jnp.where(mine == 1, analysis, 0.0)

    tables[0].wait()

    def one(f, _):
        pltpu.make_async_copy(field_hbm.at[0, 0], field.at[f], field_sem.at[f]).wait()

        @pl.when(f + window < F)
        def _():
            n = f + window
            pltpu.make_async_copy(field_hbm.at[n // levels, n % levels], field.at[n], field_sem.at[n]).start()

        high, low = split(field[f])
        wide = dot(fy[...], high)
        band = wide[:SLOTS] + wide[32 : 32 + SLOTS] + dot(fy[:32], low)[:SLOTS]
        for tile in range(bands.shape[0]):
            bands[tile, pl.ds(f, SLOTS, stride=F), :] = band[:, 128 * tile : 128 * tile + 128]
        return 0

    lax.fori_loop(0, F, one, 0)
    tables[1].wait()
    high, low = split(jnp.concatenate([bands[tile] for tile in range(bands.shape[0])], axis=1))
    both = dot(high, fx[...])
    spectrum = both[:, :128] + both[:, 128:] + dot(low, fx[:, :128])
    spectrum = pack([spectrum[F * slot : F * slot + F] for slot in range(SLOTS)])
    share[...] = factor * (analysis - spectrum)
    tables[2].wait()
    tables[3].wait()


def nudge_kernel(levels, chunk, mine, other, field, iy, ix, out_hbm, out, bands, sem):
    total = mine[...] + other[...]
    group = lane_group((F, 128))
    rows = []
    for j in range(4):
        for block in range(SLOTS // 4):
            rows.append(jnp.where(group == j, total[:, 128 * block : 128 * block + 128], 0.0))
    high, low = split(jnp.concatenate(rows, axis=0))
    wide = dot(high, ix[:128]) + dot(high, ix[128:]) + dot(low, ix[:128])
    for tile in range(bands.shape[0]):
        bands[tile] = wide[:, 128 * tile : 128 * tile + 128]
    ny, nx = out.shape[1:]
    steps = ny // chunk

    def one(f, _):
        band = [bands[tile, pl.ds(f, SLOTS, stride=F), :] for tile in range(bands.shape[0])]
        band = jnp.concatenate(band, axis=1)
        high = band.astype(jnp.bfloat16).astype(jnp.float32)
        stacked = jnp.concatenate([high, high, band - high, jnp.zeros((128 - 3 * SLOTS, nx), jnp.float32)], axis=0)
        stacked = stacked.astype(jnp.bfloat16)
        for step in range(steps):
            at = pl.ds(step * chunk, chunk)
            out[f, at] = field[f, at] + dot(iy[at], stacked)
            pltpu.make_async_copy(
                out.at[f, at], out_hbm.at[f // levels, f % levels, at], sem.at[f * steps + step]
            ).start()
        return 0

    lax.fori_loop(0, F, one, 0)

    def end(n, _):
        f, step = n // steps, n % steps
        at = pl.ds(pl.multiple_of(step * chunk, chunk), chunk)
        pltpu.make_async_copy(out.at[f, at], out_hbm.at[f // levels, f % levels, at], sem.at[n]).wait()
        return 0

    lax.fori_loop(0, F * steps, end, 0)


def in_hbm(value):
    return pltpu.with_memory_space_constraint(jnp.asarray(value), pltpu.HBM)


def swap(value, axis, size, bit):
    return lax.ppermute(value, axis, [(i, i ^ bit) for i in range(size)])


def body(n_gx, n_gy, model_state, cutoff, relax_rate, owner_map, era_store):
    nvar, levels, ny, nx = model_state.shape
    fy, fx = forward_tables(n_gx, n_gy)
    iy, ix = inverse_tables(n_gx, n_gy)
    vmem = pl.BlockSpec(memory_space=pltpu.VMEM)
    hbm = pl.BlockSpec(memory_space=pltpu.HBM)
    share, field, iy, ix = pl.pallas_call(
        functools.partial(project_kernel, n_gy, levels),
        out_shape=(
            pltpu.VMEM((F, PACKED), jnp.float32),
            pltpu.VMEM((F, ny, nx), jnp.float32),
            pltpu.VMEM((ny, 128), jnp.bfloat16),
            pltpu.VMEM((256, nx), jnp.bfloat16),
        ),
        in_specs=[hbm] * 9,
        out_specs=[vmem] * 4,
        scratch_shapes=[
            pltpu.SMEM(owner_map.shape, jnp.int32),
            pltpu.SMEM(cutoff.shape, jnp.int32),
            pltpu.SMEM(relax_rate.shape, jnp.float32),
            pltpu.VMEM(era_store.shape, jnp.float32),
            pltpu.VMEM((F, 1024), jnp.float32),
            pltpu.VMEM((64, ny), jnp.bfloat16),
            pltpu.VMEM((nx, 256), jnp.bfloat16),
            pltpu.VMEM((nx // 128, SLOTS * F, 128), jnp.float32),
            pltpu.SemaphoreType.DMA((F,)),
            pltpu.SemaphoreType.DMA((4,)),
            pltpu.SemaphoreType.DMA((4,)),
        ],
        compiler_params=pltpu.CompilerParams(vmem_limit_bytes=20 * 2**20),
        name="project",
    )(*(in_hbm(value) for value in (owner_map, cutoff, relax_rate, era_store, model_state, fy, fx, iy, ix)))

    steps = [("gx", n_gx, 1 << bit) for bit in range(n_gx.bit_length() - 1)]
    steps += [("gy", n_gy, 1 << bit) for bit in range(n_gy.bit_length() - 1)]
    for step in steps[:-1]:
        share = share + swap(share, *step)
    other = swap(share, *steps[-1])

    chunk = min(ny, 256)
    nudged = pl.pallas_call(
        functools.partial(nudge_kernel, levels, chunk),
        out_shape=jax.ShapeDtypeStruct(model_state.shape, jnp.float32),
        in_specs=[vmem] * 5,
        out_specs=hbm,
        scratch_shapes=[
            pltpu.VMEM((F, ny, nx), jnp.float32),
            pltpu.VMEM((nx // 128, SLOTS * F, 128), jnp.float32),
            pltpu.SemaphoreType.DMA((F * (ny // chunk),)),
        ],
        compiler_params=pltpu.CompilerParams(vmem_limit_bytes=30 * 2**20),
        name="nudge",
    )(share, other, field, iy, ix)
    return nudged


def solution(mesh):
    n_gx, n_gy = mesh.shape["gx"], mesh.shape["gy"]
    placed = (
        P(None, "lev", "gy", "gx"),
        P(None, "lev"),
        P(None, "lev"),
        P("lev", None),
        P(("gx", "gy"), None, "lev", None),
    )
    return jax.shard_map(
        functools.partial(body, n_gx, n_gy),
        mesh=mesh,
        in_specs=placed,
        out_specs=P(None, "lev", "gy", "gx"),
        check_vma=False,
    )
```

```python
import functools

import jax
import jax.numpy as jnp
import ml_dtypes
import numpy as np
from jax import lax
from jax.experimental import pallas as pl
from jax.experimental.pallas import tpu as pltpu
from jax.sharding import PartitionSpec as P

NX = 2048
NY = 2048
KC = 10
NK = 21
F = 8
GROUP = 32
SLOTS = 24
PACKED = SLOTS * GROUP


def basis(positions, length):
    wave = np.concatenate([np.arange(KC + 1), np.arange(1, KC + 1)])
    angle = np.mod(positions[:, None] * wave[None, :], length) * (2 * np.pi / length)
    return np.where(np.arange(NK) <= KC, np.cos(angle), np.sin(angle))


def halves(table):
    high = table.astype(ml_dtypes.bfloat16)
    low = (table - high.astype(np.float64)).astype(ml_dtypes.bfloat16)
    return high, low


def forward_tables(n_gx, n_gy):
    weight = np.where(np.arange(NK) == 0, 1.0, 2.0)
    high, low = halves(basis(np.arange(NY), NY) * weight / NY)
    ny = NY // n_gy
    along_y = np.zeros((n_gy, 64, ny), ml_dtypes.bfloat16)
    along_y[:, :NK] = high.reshape(n_gy, ny, NK).transpose(0, 2, 1)
    along_y[:, 32 : 32 + NK] = low.reshape(n_gy, ny, NK).transpose(0, 2, 1)
    high, low = halves(basis(np.arange(NX), NX) * weight / NX)
    nx = NX // n_gx
    along_x = np.zeros((n_gx, nx, 256), ml_dtypes.bfloat16)
    for group in range(4):
        at = group * GROUP
        along_x[:, :, at : at + NK] = high.reshape(n_gx, nx, NK)
        along_x[:, :, 128 + at : 128 + at + NK] = low.reshape(n_gx, nx, NK)
    return along_y, along_x


def inverse_tables(n_gx, n_gy):
    high, low = halves(basis(np.arange(NY), NY))
    ny = NY // n_gy
    along_y = np.zeros((n_gy, ny, 128), ml_dtypes.bfloat16)
    for slot in range(NK):
        at = (slot % 4) * (SLOTS // 4) + slot // 4
        along_y[:, :, at] = high[:, slot].reshape(n_gy, ny)
        along_y[:, :, SLOTS + at] = low[:, slot].reshape(n_gy, ny)
        along_y[:, :, 2 * SLOTS + at] = high[:, slot].reshape(n_gy, ny)
    high, low = halves(basis(np.arange(NX), NX))
    nx = NX // n_gx
    along_x = np.zeros((n_gx, 256, nx), ml_dtypes.bfloat16)
    for group in range(4):
        at = group * GROUP
        along_x[:, at : at + NK] = high.reshape(n_gx, nx, NK).transpose(0, 2, 1)
        along_x[:, 128 + at : 128 + at + NK] = low.reshape(n_gx, nx, NK).transpose(0, 2, 1)
    return along_y, along_x


def split(value):
    high = value.astype(jnp.bfloat16)
    return high, (value - high.astype(jnp.float32)).astype(jnp.bfloat16)


def dot(left, right):
    return jnp.dot(left, right, preferred_element_type=jnp.float32)


def lane_group(shape):
    return lax.broadcasted_iota(jnp.int32, shape, 1) // GROUP


def analysis_rows(store):
    pieces = []
    for row in range(2 * NK):
        at = row * NK
        base = at // 128 * 128
        off = at - base
        width = 128 if off + NK <= 128 else 256
        window = store[:, base : base + width]
        pieces.append(pltpu.roll(window, (width - off) % width, 1)[:, :128] if off else window[:, :128])
    high, low = split(jnp.concatenate(pieces, axis=0))
    wave = lax.broadcasted_iota(jnp.int32, (128, 128), 0) - KC
    column = lax.broadcasted_iota(jnp.int32, (128, 128), 1) % GROUP
    number = jnp.where(column <= KC, column, column - KC)
    plus = jnp.where(wave == number, 1.0, 0.0)
    minus = jnp.where((wave == -number) & (number > 0), 1.0, 0.0)
    fold = jnp.where(column <= KC, plus + minus, plus - minus)
    fold = jnp.where(column < NK, fold, 0.0).astype(jnp.bfloat16)
    folded = dot(high, fold) + dot(low, fold)
    part = [folded[8 * row : 8 * row + 8] for row in range(2 * NK)]
    real, imag = part[:NK], part[NK:]
    even = lax.broadcasted_iota(jnp.int32, (8, 128), 1) % GROUP <= KC
    rows = [jnp.where(even, real[KC], -imag[KC])]
    for wave in range(1, KC + 1):
        up, down = KC + wave, KC - wave
        rows.append(jnp.where(even, real[up] + real[down], -(imag[up] + imag[down])))
    for wave in range(1, KC + 1):
        up, down = KC + wave, KC - wave
        rows.append(-jnp.where(even, imag[up] - imag[down], real[up] - real[down]))
    return rows


def pack(rows):
    group = lane_group((8, 128))
    blocks = []
    for block in range(SLOTS // 4):
        total = jnp.zeros((8, 128), jnp.float32)
        for j in range(4):
            if 4 * block + j < len(rows):
                total = jnp.where(group == j, rows[4 * block + j], total)
        blocks.append(total)
    return jnp.concatenate(blocks, axis=1)


def per_field(values):
    row = lax.broadcasted_iota(jnp.int32, (F, 1), 0)
    total = jnp.full((F, 1), values[0])
    for field in range(1, F):
        total = jnp.where(row == field, values[field], total)
    return total


def project_kernel(
    n_gy, levels, owner_hbm, cutoff_hbm, relax_hbm, era_hbm, field_hbm, fy_hbm, fx_hbm, iy_hbm, ix_hbm,
    share, field, iy, ix, owner, cutoff, relax, era, store, fy, fx, bands, field_sem, small_sem, table_sem,
):
    gx, gy = lax.axis_index("gx"), lax.axis_index("gy")
    tables = [
        pltpu.make_async_copy(src, dst, table_sem.at[n])
        for n, (src, dst) in enumerate(
            ((fy_hbm.at[gy], fy), (fx_hbm.at[gx], fx), (iy_hbm.at[gy], iy), (ix_hbm.at[gx], ix))
        )
    ]
    small = [
        pltpu.make_async_copy(src, dst, small_sem.at[n])
        for n, (src, dst) in enumerate(
            ((era_hbm, era), (owner_hbm, owner), (cutoff_hbm, cutoff), (relax_hbm, relax))
        )
    ]
    for copy in small:
        copy.start()
    tables[0].start()
    def load(f, _):
        pltpu.make_async_copy(field_hbm.at[f // levels, f % levels], field.at[f], field_sem.at[f]).start()
        return 0

    lax.fori_loop(0, F, load, 0)
    for copy in tables[1:]:
        copy.start()

    store[...] = jnp.zeros_like(store)
    for copy in small:
        copy.wait()
    for var in range(F // levels):
        store[var * levels : (var + 1) * levels, : 2 * NK * NK] = era[0, var]
    analysis = pack(analysis_rows(store[...]))
    me = gx * n_gy + gy
    mine = per_field([(owner[0, f // levels] == me).astype(jnp.int32) for f in range(F)])
    limit = per_field([cutoff[f // levels, f % levels] for f in range(F)])
    rate = per_field([relax[f // levels, f % levels] for f in range(F)])
    lane = lax.broadcasted_iota(jnp.int32, (F, PACKED), 1)
    slot, column = lane // GROUP, lane % GROUP
    ky = jnp.where(slot <= KC, slot, slot - KC)
    kx = jnp.where(column <= KC, column, column - KC)
    factor = jnp.where(ky * ky + kx * kx <= limit * limit, rate, 0.0)
    analysis = jnp.where(mine == 1, analysis, 0.0)

    tables[0].wait()

    def one(f, _):
        pltpu.make_async_copy(field_hbm.at[0, 0], field.at[f], field_sem.at[f]).wait()

        high, low = split(field[f])
        wide = dot(fy[...], high)
        band = wide[:SLOTS] + wide[32 : 32 + SLOTS] + dot(fy[:32], low)[:SLOTS]
        for tile in range(bands.shape[0]):
            bands[tile, pl.ds(f, SLOTS, stride=F), :] = band[:, 128 * tile : 128 * tile + 128]
        return 0

    lax.fori_loop(0, F, one, 0)
    tables[1].wait()
    high, low = split(jnp.concatenate([bands[tile] for tile in range(bands.shape[0])], axis=1))
    both = dot(high, fx[...])
    spectrum = both[:, :128] + both[:, 128:] + dot(low, fx[:, :128])
    spectrum = pack([spectrum[F * slot : F * slot + F] for slot in range(SLOTS)])
    share[...] = factor * (analysis - spectrum)
    tables[2].wait()
    tables[3].wait()


def nudge_kernel(levels, chunk, mine, other, field, iy, ix, out_hbm, out, bands, sem):
    total = mine[...] + other[...]
    group = lane_group((F, 128))
    rows = []
    for j in range(4):
        for block in range(SLOTS // 4):
            rows.append(jnp.where(group == j, total[:, 128 * block : 128 * block + 128], 0.0))
    high, low = split(jnp.concatenate(rows, axis=0))
    wide = dot(high, ix[:128]) + dot(high, ix[128:]) + dot(low, ix[:128])
    for tile in range(bands.shape[0]):
        bands[tile] = wide[:, 128 * tile : 128 * tile + 128]
    ny, nx = out.shape[1:]
    steps = ny // chunk

    def one(f, _):
        band = [bands[tile, pl.ds(f, SLOTS, stride=F), :] for tile in range(bands.shape[0])]
        band = jnp.concatenate(band, axis=1)
        high = band.astype(jnp.bfloat16).astype(jnp.float32)
        stacked = jnp.concatenate([high, high, band - high, jnp.zeros((128 - 3 * SLOTS, nx), jnp.float32)], axis=0)
        stacked = stacked.astype(jnp.bfloat16)
        for step in range(steps):
            at = pl.ds(step * chunk, chunk)
            out[f, at] = field[f, at] + dot(iy[at], stacked)
            pltpu.make_async_copy(
                out.at[f, at], out_hbm.at[f // levels, f % levels, at], sem.at[f * steps + step]
            ).start()
        return 0

    lax.fori_loop(0, F, one, 0)

    def end(n, _):
        f, step = n // steps, n % steps
        at = pl.ds(pl.multiple_of(step * chunk, chunk), chunk)
        pltpu.make_async_copy(out.at[f, at], out_hbm.at[f // levels, f % levels, at], sem.at[n]).wait()
        return 0

    lax.fori_loop(0, F * steps, end, 0)


def in_hbm(value):
    return pltpu.with_memory_space_constraint(jnp.asarray(value), pltpu.HBM)


def phases_of(n_gx, n_gy):
    along_y = [[1 << bit] for bit in range(n_gy.bit_length() - 1)]
    along_x = [[bits * n_gy for bits in range(1, min(n_gx, 4))]]
    along_x += [[n_gy << bit] for bit in range(2, n_gx.bit_length() - 1)]
    return along_y[:1] + along_x + along_y[1:]


def swap(value, size, bits):
    return lax.ppermute(value, ("gx", "gy"), [(i, i ^ bits) for i in range(size)])


def body(n_gx, n_gy, model_state, cutoff, relax_rate, owner_map, era_store):
    nvar, levels, ny, nx = model_state.shape
    fy, fx = forward_tables(n_gx, n_gy)
    iy, ix = inverse_tables(n_gx, n_gy)
    vmem = pl.BlockSpec(memory_space=pltpu.VMEM)
    hbm = pl.BlockSpec(memory_space=pltpu.HBM)
    share, field, iy, ix = pl.pallas_call(
        functools.partial(project_kernel, n_gy, levels),
        out_shape=(
            pltpu.VMEM((F, PACKED), jnp.float32),
            pltpu.VMEM((F, ny, nx), jnp.float32),
            pltpu.VMEM((ny, 128), jnp.bfloat16),
            pltpu.VMEM((256, nx), jnp.bfloat16),
        ),
        in_specs=[hbm] * 9,
        out_specs=[vmem] * 4,
        scratch_shapes=[
            pltpu.SMEM(owner_map.shape, jnp.int32),
            pltpu.SMEM(cutoff.shape, jnp.int32),
            pltpu.SMEM(relax_rate.shape, jnp.float32),
            pltpu.VMEM(era_store.shape, jnp.float32),
            pltpu.VMEM((F, 1024), jnp.float32),
            pltpu.VMEM((64, ny), jnp.bfloat16),
            pltpu.VMEM((nx, 256), jnp.bfloat16),
            pltpu.VMEM((nx // 128, SLOTS * F, 128), jnp.float32),
            pltpu.SemaphoreType.DMA((F,)),
            pltpu.SemaphoreType.DMA((4,)),
            pltpu.SemaphoreType.DMA((4,)),
        ],
        compiler_params=pltpu.CompilerParams(vmem_limit_bytes=20 * 2**20),
        name="project",
    )(*(in_hbm(value) for value in (owner_map, cutoff, relax_rate, era_store, model_state, fy, fx, iy, ix)))

    phases = phases_of(n_gx, n_gy)
    for phase in phases[:-1]:
        got = [swap(share, n_gx * n_gy, bits) for bits in phase]
        for other in got:
            share = share + other
    other = sum(swap(share, n_gx * n_gy, bits) for bits in phases[-1])

    chunk = min(ny, 256)
    nudged = pl.pallas_call(
        functools.partial(nudge_kernel, levels, chunk),
        out_shape=jax.ShapeDtypeStruct(model_state.shape, jnp.float32),
        in_specs=[vmem] * 5,
        out_specs=hbm,
        scratch_shapes=[
            pltpu.VMEM((F, ny, nx), jnp.float32),
            pltpu.VMEM((nx // 128, SLOTS * F, 128), jnp.float32),
            pltpu.SemaphoreType.DMA((F * (ny // chunk),)),
        ],
        compiler_params=pltpu.CompilerParams(vmem_limit_bytes=30 * 2**20),
        name="nudge",
    )(share, other, field, iy, ix)
    return nudged


def solution(mesh):
    n_gx, n_gy = mesh.shape["gx"], mesh.shape["gy"]
    placed = (
        P(None, "lev", "gy", "gx"),
        P(None, "lev"),
        P(None, "lev"),
        P("lev", None),
        P(("gx", "gy"), None, "lev", None),
    )
    return jax.shard_map(
        functools.partial(body, n_gx, n_gy),
        mesh=mesh,
        in_specs=placed,
        out_specs=P(None, "lev", "gy", "gx"),
        check_vma=False,
    )
```

```python
import functools

import jax
import jax.numpy as jnp
import ml_dtypes
import numpy as np
from jax import lax
from jax.experimental import pallas as pl
from jax.experimental.pallas import tpu as pltpu
from jax.sharding import PartitionSpec as P

NX = 2048
NY = 2048
KC = 10
NK = 21
F = 8
GROUP = 32
FRONT = 16
SLOTS = 24
PACKED = FRONT * GROUP
BACK_FROM = {1: 19, 2: 23, 3: 23, 4: 31, 5: 31}


def basis(positions, length):
    order = np.arange(NK)
    angle = np.mod(positions[:, None] * ((order + 1) // 2)[None, :], length) * (2 * np.pi / length)
    return np.where((order == 0) | (order % 2 == 1), np.cos(angle), np.sin(angle))


def halves(table):
    high = table.astype(ml_dtypes.bfloat16)
    low = (table - high.astype(np.float64)).astype(ml_dtypes.bfloat16)
    return high, low


def both_ways(high, low):
    table = np.zeros((high.shape[0], 8, GROUP), ml_dtypes.bfloat16)
    for group in range(4):
        half = low if group % 2 else high
        table[:, group, :NK] = half
        table[:, 4 + group, GROUP - NK :] = half[:, ::-1]
    return table.reshape(-1, 256)


def forward_tables(n_gx, n_gy):
    weight = np.where(np.arange(NK) == 0, 1.0, 2.0)
    high, low = halves(basis(np.arange(NY), NY) * weight / NY)
    ny = NY // n_gy
    along_y = np.zeros((n_gy, 64, ny), ml_dtypes.bfloat16)
    along_y[:, :NK] = high.reshape(n_gy, ny, NK).transpose(0, 2, 1)
    along_y[:, 32 : 32 + NK] = low.reshape(n_gy, ny, NK).transpose(0, 2, 1)
    high, low = halves(basis(np.arange(NX), NX) * weight / NX)
    nx = NX // n_gx
    along_x = both_ways(high, low).reshape(n_gx, nx, 256)
    return along_y, along_x


def inverse_tables(n_gx, n_gy):
    high, low = halves(basis(np.arange(NY), NY))
    ny = NY // n_gy
    along_y = np.zeros((n_gy, ny, 128), ml_dtypes.bfloat16)
    for first, half in ((0, high), (SLOTS, low), (2 * SLOTS, high)):
        along_y[:, :, first : first + NK] = half.reshape(n_gy, ny, NK)
    high, low = halves(basis(np.arange(NX), NX))
    nx = NX // n_gx
    along_x = both_ways(high, low).reshape(n_gx, nx, 256).transpose(0, 2, 1)
    return along_y, along_x


def split(value):
    high = value.astype(jnp.bfloat16)
    return high, (value - high.astype(jnp.float32)).astype(jnp.bfloat16)


def dot(left, right):
    return jnp.dot(left, right, preferred_element_type=jnp.float32)


def lanes_of(shape):
    lane = lax.broadcasted_iota(jnp.int32, shape, 1)
    return lane // GROUP, lane % GROUP


def analysis_rows(store):
    pieces = []
    for row in range(2 * NK):
        at = row * NK
        base = at // 128 * 128
        off = at - base
        width = 128 if off + NK <= 128 else 256
        window = store[:, base : base + width]
        pieces.append(pltpu.roll(window, (width - off) % width, 1)[:, :128] if off else window[:, :128])
    high, low = split(jnp.concatenate(pieces, axis=0))
    wave = lax.broadcasted_iota(jnp.int32, (128, 256), 0) - KC
    group, column = lanes_of((128, 256))
    column = jnp.where(group < 4, column, GROUP - 1 - column)
    number = (column + 1) // 2
    plus = jnp.where(wave == number, 1.0, 0.0)
    minus = jnp.where((wave == -number) & (number > 0), 1.0, 0.0)
    fold = jnp.where(column % 2 == 1, plus + minus, plus - minus)
    fold = jnp.where(column < NK, fold, 0.0).astype(jnp.bfloat16)
    folded = dot(high, fold) + dot(low, fold)
    column = lanes_of((8, 128))[1]
    rows = []
    for slot in range(NK):
        wave, back = (slot + 1) // 2, slot >= FRONT
        lanes = slice(128, 256) if back else slice(0, 128)
        along = GROUP - 1 - column if back else column
        even = (along == 0) | (along % 2 == 1)
        up, down = KC + wave, KC - wave
        real_up, real_down = (folded[8 * row : 8 * row + 8, lanes] for row in (up, down))
        imag_up, imag_down = (folded[8 * row : 8 * row + 8, lanes] for row in (NK + up, NK + down))
        if wave == 0:
            rows.append(jnp.where(even, real_up, -imag_up))
        elif slot % 2:
            rows.append(jnp.where(even, real_up + real_down, -(imag_up + imag_down)))
        else:
            rows.append(-jnp.where(even, imag_up - imag_down, real_up - real_down))
    return rows


def pack(rows):
    group, column = lanes_of((8, 128))
    blocks = []
    for block in range(FRONT // 4):
        total = jnp.zeros((8, 128), jnp.float32)
        for j in range(4):
            at = 4 * block + j
            total = jnp.where(group == j, rows[at], total)
            if at in BACK_FROM:
                total = jnp.where((group == j) & (column >= BACK_FROM[at]), rows[at + FRONT - 1], total)
        blocks.append(total)
    return jnp.concatenate(blocks, axis=1)


def unpack(packed):
    group, column = lanes_of((8, 128))
    zero = jnp.zeros((8, 128), jnp.float32)
    rows = [None] * SLOTS
    for block in range(FRONT // 4):
        here = packed[:, 128 * block : 128 * block + 128]
        after = pltpu.roll(here, GROUP, 1)
        for j in range(4):
            at = 4 * block + j
            row = jnp.where(group == j, here, jnp.where(group == (j + 1) % 4, after, 0.0))
            if at in BACK_FROM:
                back = column >= BACK_FROM[at]
                rows[at + FRONT - 1] = jnp.concatenate([zero, jnp.where(back, row, 0.0)], axis=1)
                row = jnp.where(back, 0.0, row)
            rows[at] = jnp.concatenate([row, zero], axis=1)
    empty = jnp.zeros((8, 256), jnp.float32)
    return jnp.concatenate([empty if row is None else row for row in rows], axis=0)


def per_field(values):
    row = lax.broadcasted_iota(jnp.int32, (F, 1), 0)
    total = jnp.full((F, 1), values[0])
    for field in range(1, F):
        total = jnp.where(row == field, values[field], total)
    return total


def project_kernel(
    n_gy, levels, owner_hbm, cutoff_hbm, relax_hbm, era_hbm, field_hbm, fy_hbm, fx_hbm, iy_hbm, ix_hbm,
    share, field, iy, ix, owner, cutoff, relax, era, store, fy, fx, bands, field_sem, small_sem, table_sem,
):
    gx, gy = lax.axis_index("gx"), lax.axis_index("gy")
    tables = [
        pltpu.make_async_copy(src, dst, table_sem.at[n])
        for n, (src, dst) in enumerate(
            ((fy_hbm.at[gy], fy), (fx_hbm.at[gx], fx), (iy_hbm.at[gy], iy), (ix_hbm.at[gx], ix))
        )
    ]
    small = [
        pltpu.make_async_copy(src, dst, small_sem.at[n])
        for n, (src, dst) in enumerate(
            ((era_hbm, era), (owner_hbm, owner), (cutoff_hbm, cutoff), (relax_hbm, relax))
        )
    ]
    for copy in small:
        copy.start()
    tables[0].start()
    def load(f, _):
        pltpu.make_async_copy(field_hbm.at[f // levels, f % levels], field.at[f], field_sem.at[f]).start()
        return 0

    lax.fori_loop(0, F, load, 0)
    for copy in tables[1:]:
        copy.start()

    store[...] = jnp.zeros_like(store)
    for copy in small:
        copy.wait()
    for var in range(F // levels):
        store[var * levels : (var + 1) * levels, : 2 * NK * NK] = era[0, var]
    analysis = pack(analysis_rows(store[...]))
    me = gx * n_gy + gy
    mine = per_field([(owner[0, f // levels] == me).astype(jnp.int32) for f in range(F)])
    limit = per_field([cutoff[f // levels, f % levels] for f in range(F)])
    rate = per_field([relax[f // levels, f % levels] for f in range(F)])
    group, column = lanes_of((F, PACKED))
    start = jnp.full((F, PACKED), GROUP)
    for at, first in BACK_FROM.items():
        start = jnp.where(group == at, first, start)
    back = column >= start
    ky = jnp.where(back, group + FRONT, group + 1) // 2
    kx = jnp.where(back, GROUP - column, column + 1) // 2
    factor = jnp.where(ky * ky + kx * kx <= limit * limit, rate, 0.0)
    analysis = jnp.where(mine == 1, analysis, 0.0)

    tables[0].wait()

    def one(f, _):
        pltpu.make_async_copy(field_hbm.at[0, 0], field.at[f], field_sem.at[f]).wait()

        high, low = split(field[f])
        wide = dot(fy[...], high)
        band = wide[:SLOTS] + wide[32 : 32 + SLOTS] + dot(fy[:32], low)[:SLOTS]
        for tile in range(bands.shape[0]):
            bands[tile, pl.ds(f, SLOTS, stride=F), :] = band[:, 128 * tile : 128 * tile + 128]
        return 0

    lax.fori_loop(0, F, one, 0)
    tables[1].wait()
    high, low = split(jnp.concatenate([bands[tile] for tile in range(bands.shape[0])], axis=1))
    both = dot(high, fx[...]) + dot(low, fx[...])
    both = [both[:, 128 * way : 128 * way + 128] for way in range(2)]
    both = [way + pltpu.roll(way, 128 - GROUP, 1) for way in both]
    spectrum = pack([both[int(slot >= FRONT)][F * slot : F * slot + F] for slot in range(NK)])
    share[...] = factor * (analysis - spectrum)
    tables[2].wait()
    tables[3].wait()


def nudge_kernel(levels, chunk, mine, other, field, iy, ix, out_hbm, out, bands, sem):
    high, low = split(unpack(mine[...] + other[...]))
    wide = dot(high, ix[...]) + dot(low, ix[...])
    for tile in range(bands.shape[0]):
        bands[tile] = wide[:, 128 * tile : 128 * tile + 128]
    ny, nx = out.shape[1:]
    steps = ny // chunk

    def one(f, _):
        band = [bands[tile, pl.ds(f, SLOTS, stride=F), :] for tile in range(bands.shape[0])]
        band = jnp.concatenate(band, axis=1)
        high = band.astype(jnp.bfloat16).astype(jnp.float32)
        stacked = jnp.concatenate([high, high, band - high, jnp.zeros((128 - 3 * SLOTS, nx), jnp.float32)], axis=0)
        stacked = stacked.astype(jnp.bfloat16)
        for step in range(steps):
            at = pl.ds(step * chunk, chunk)
            out[f, at] = field[f, at] + dot(iy[at], stacked)
            pltpu.make_async_copy(
                out.at[f, at], out_hbm.at[f // levels, f % levels, at], sem.at[f * steps + step]
            ).start()
        return 0

    lax.fori_loop(0, F, one, 0)

    def end(n, _):
        f, step = n // steps, n % steps
        at = pl.ds(pl.multiple_of(step * chunk, chunk), chunk)
        pltpu.make_async_copy(out.at[f, at], out_hbm.at[f // levels, f % levels, at], sem.at[n]).wait()
        return 0

    lax.fori_loop(0, F * steps, end, 0)


def in_hbm(value):
    return pltpu.with_memory_space_constraint(jnp.asarray(value), pltpu.HBM)


def phases_of(n_gx, n_gy):
    along_y = [[1 << bit] for bit in range(n_gy.bit_length() - 1)]
    along_x = [[bits * n_gy for bits in range(1, min(n_gx, 4))]]
    along_x += [[n_gy << bit] for bit in range(2, n_gx.bit_length() - 1)]
    return along_y[:1] + along_x + along_y[1:]


def swap(value, size, bits):
    return lax.ppermute(value, ("gx", "gy"), [(i, i ^ bits) for i in range(size)])


def body(n_gx, n_gy, model_state, cutoff, relax_rate, owner_map, era_store):
    nvar, levels, ny, nx = model_state.shape
    fy, fx = forward_tables(n_gx, n_gy)
    iy, ix = inverse_tables(n_gx, n_gy)
    vmem = pl.BlockSpec(memory_space=pltpu.VMEM)
    hbm = pl.BlockSpec(memory_space=pltpu.HBM)
    share, field, iy, ix = pl.pallas_call(
        functools.partial(project_kernel, n_gy, levels),
        out_shape=(
            pltpu.VMEM((F, PACKED), jnp.float32),
            pltpu.VMEM((F, ny, nx), jnp.float32),
            pltpu.VMEM((ny, 128), jnp.bfloat16),
            pltpu.VMEM((256, nx), jnp.bfloat16),
        ),
        in_specs=[hbm] * 9,
        out_specs=[vmem] * 4,
        scratch_shapes=[
            pltpu.SMEM(owner_map.shape, jnp.int32),
            pltpu.SMEM(cutoff.shape, jnp.int32),
            pltpu.SMEM(relax_rate.shape, jnp.float32),
            pltpu.VMEM(era_store.shape, jnp.float32),
            pltpu.VMEM((F, 1024), jnp.float32),
            pltpu.VMEM((64, ny), jnp.bfloat16),
            pltpu.VMEM((nx, 256), jnp.bfloat16),
            pltpu.VMEM((nx // 128, SLOTS * F, 128), jnp.float32),
            pltpu.SemaphoreType.DMA((F,)),
            pltpu.SemaphoreType.DMA((4,)),
            pltpu.SemaphoreType.DMA((4,)),
        ],
        compiler_params=pltpu.CompilerParams(vmem_limit_bytes=20 * 2**20),
        name="project",
    )(*(in_hbm(value) for value in (owner_map, cutoff, relax_rate, era_store, model_state, fy, fx, iy, ix)))

    phases = phases_of(n_gx, n_gy)
    for phase in phases[:-1]:
        got = [swap(share, n_gx * n_gy, bits) for bits in phase]
        for other in got:
            share = share + other
    other = sum(swap(share, n_gx * n_gy, bits) for bits in phases[-1])

    chunk = min(ny, 256)
    nudged = pl.pallas_call(
        functools.partial(nudge_kernel, levels, chunk),
        out_shape=jax.ShapeDtypeStruct(model_state.shape, jnp.float32),
        in_specs=[vmem] * 5,
        out_specs=hbm,
        scratch_shapes=[
            pltpu.VMEM((F, ny, nx), jnp.float32),
            pltpu.VMEM((nx // 128, SLOTS * F, 128), jnp.float32),
            pltpu.SemaphoreType.DMA((F * (ny // chunk),)),
        ],
        compiler_params=pltpu.CompilerParams(vmem_limit_bytes=30 * 2**20),
        name="nudge",
    )(share, other, field, iy, ix)
    return nudged


def solution(mesh):
    n_gx, n_gy = mesh.shape["gx"], mesh.shape["gy"]
    placed = (
        P(None, "lev", "gy", "gx"),
        P(None, "lev"),
        P(None, "lev"),
        P("lev", None),
        P(("gx", "gy"), None, "lev", None),
    )
    return jax.shard_map(
        functools.partial(body, n_gx, n_gy),
        mesh=mesh,
        in_specs=placed,
        out_specs=P(None, "lev", "gy", "gx"),
        check_vma=False,
    )
```

```python
import functools

import jax
import jax.numpy as jnp
import ml_dtypes
import numpy as np
from jax import lax
from jax.experimental import pallas as pl
from jax.experimental.pallas import tpu as pltpu
from jax.sharding import PartitionSpec as P

NX = 2048
NY = 2048
KC = 10
NK = 21
F = 8
GROUP = 32
FRONT = 16
SLOTS = 24
PACKED = FRONT * GROUP
BACK_FROM = {1: 19, 2: 23, 3: 23, 4: 31, 5: 31}


def basis(positions, length):
    order = np.arange(NK)
    angle = np.mod(positions[:, None] * ((order + 1) // 2)[None, :], length) * (2 * np.pi / length)
    return np.where((order == 0) | (order % 2 == 1), np.cos(angle), np.sin(angle))


def halves(table):
    high = table.astype(ml_dtypes.bfloat16)
    low = (table - high.astype(np.float64)).astype(ml_dtypes.bfloat16)
    return high, low


def both_ways(high, low):
    table = np.zeros((high.shape[0], 8, GROUP), ml_dtypes.bfloat16)
    for group in range(4):
        half = low if group % 2 else high
        table[:, group, :NK] = half
        table[:, 4 + group, GROUP - NK :] = half[:, ::-1]
    return table.reshape(-1, 256)


def forward_tables(n_gx, n_gy):
    weight = np.where(np.arange(NK) == 0, 1.0, 2.0)
    high, low = halves(basis(np.arange(NY), NY) * weight / NY)
    ny = NY // n_gy
    along_y = np.zeros((n_gy, 64, ny), ml_dtypes.bfloat16)
    along_y[:, :NK] = high.reshape(n_gy, ny, NK).transpose(0, 2, 1)
    along_y[:, 32 : 32 + NK] = low.reshape(n_gy, ny, NK).transpose(0, 2, 1)
    high, low = halves(basis(np.arange(NX), NX) * weight / NX)
    nx = NX // n_gx
    along_x = both_ways(high, low).reshape(n_gx, nx, 256)
    return along_y, along_x


def inverse_tables(n_gx, n_gy):
    high, low = halves(basis(np.arange(NY), NY))
    ny = NY // n_gy
    along_y = np.zeros((n_gy, ny, 128), ml_dtypes.bfloat16)
    for first, half in ((0, high), (SLOTS, low), (2 * SLOTS, high)):
        along_y[:, :, first : first + NK] = half.reshape(n_gy, ny, NK)
    high, low = halves(basis(np.arange(NX), NX))
    nx = NX // n_gx
    along_x = both_ways(high, low).reshape(n_gx, nx, 256).transpose(0, 2, 1)
    return along_y, along_x


def split(value):
    high = value.astype(jnp.bfloat16)
    return high, (value - high.astype(jnp.float32)).astype(jnp.bfloat16)


def dot(left, right):
    return jnp.dot(left, right, preferred_element_type=jnp.float32)


def lanes_of(shape):
    lane = lax.broadcasted_iota(jnp.int32, shape, 1)
    return lane // GROUP, lane % GROUP


def analysis_rows(store):
    pieces = []
    for row in range(2 * NK):
        at = row * NK
        base = at // 128 * 128
        off = at - base
        width = 128 if off + NK <= 128 else 256
        window = store[:, base : base + width]
        pieces.append(pltpu.roll(window, (width - off) % width, 1)[:, :128] if off else window[:, :128])
    high, low = split(jnp.concatenate(pieces, axis=0))
    wave = lax.broadcasted_iota(jnp.int32, (128, 256), 0) - KC
    group, column = lanes_of((128, 256))
    column = jnp.where(group < 4, column, GROUP - 1 - column)
    number = (column + 1) // 2
    plus = jnp.where(wave == number, 1.0, 0.0)
    minus = jnp.where((wave == -number) & (number > 0), 1.0, 0.0)
    fold = jnp.where(column % 2 == 1, plus + minus, plus - minus)
    fold = jnp.where(column < NK, fold, 0.0).astype(jnp.bfloat16)
    folded = dot(high, fold) + dot(low, fold)
    column = lanes_of((8, 128))[1]
    rows = []
    for slot in range(NK):
        wave, back = (slot + 1) // 2, slot >= FRONT
        lanes = slice(128, 256) if back else slice(0, 128)
        along = GROUP - 1 - column if back else column
        even = (along == 0) | (along % 2 == 1)
        up, down = KC + wave, KC - wave
        real_up, real_down = (folded[8 * row : 8 * row + 8, lanes] for row in (up, down))
        imag_up, imag_down = (folded[8 * row : 8 * row + 8, lanes] for row in (NK + up, NK + down))
        if wave == 0:
            rows.append(jnp.where(even, real_up, -imag_up))
        elif slot % 2:
            rows.append(jnp.where(even, real_up + real_down, -(imag_up + imag_down)))
        else:
            rows.append(-jnp.where(even, imag_up - imag_down, real_up - real_down))
    return rows


def pack(rows):
    group, column = lanes_of((8, 128))
    blocks = []
    for block in range(FRONT // 4):
        total = jnp.zeros((8, 128), jnp.float32)
        for j in range(4):
            at = 4 * block + j
            total = jnp.where(group == j, rows[at], total)
            if at in BACK_FROM:
                total = jnp.where((group == j) & (column >= BACK_FROM[at]), rows[at + FRONT - 1], total)
        blocks.append(total)
    return jnp.concatenate(blocks, axis=1)


def unpack(packed):
    group, column = lanes_of((8, 128))
    zero = jnp.zeros((8, 128), jnp.float32)
    rows = [None] * SLOTS
    for block in range(FRONT // 4):
        here = packed[:, 128 * block : 128 * block + 128]
        after = pltpu.roll(here, GROUP, 1)
        for j in range(4):
            at = 4 * block + j
            row = jnp.where(group == j, here, jnp.where(group == (j + 1) % 4, after, 0.0))
            if at in BACK_FROM:
                back = column >= BACK_FROM[at]
                rows[at + FRONT - 1] = jnp.concatenate([zero, jnp.where(back, row, 0.0)], axis=1)
                row = jnp.where(back, 0.0, row)
            rows[at] = jnp.concatenate([row, zero], axis=1)
    empty = jnp.zeros((8, 256), jnp.float32)
    return jnp.concatenate([empty if row is None else row for row in rows], axis=0)


def per_field(values):
    row = lax.broadcasted_iota(jnp.int32, (F, 1), 0)
    total = jnp.full((F, 1), values[0])
    for field in range(1, F):
        total = jnp.where(row == field, values[field], total)
    return total


def project_kernel(
    n_gy, levels, owner_hbm, cutoff_hbm, relax_hbm, era_hbm, field_hbm, fy_hbm, fx_hbm, iy_hbm, ix_hbm,
    share, field, iy, ix, owner, cutoff, relax, era, store, fy, fx, bands, field_sem, small_sem, table_sem,
):
    gx, gy = lax.axis_index("gx"), lax.axis_index("gy")
    tables = [
        pltpu.make_async_copy(src, dst, table_sem.at[n])
        for n, (src, dst) in enumerate(
            ((fy_hbm.at[gy], fy), (fx_hbm.at[gx], fx), (iy_hbm.at[gy], iy), (ix_hbm.at[gx], ix))
        )
    ]
    small = [
        pltpu.make_async_copy(src, dst, small_sem.at[n])
        for n, (src, dst) in enumerate(
            ((era_hbm, era), (owner_hbm, owner), (cutoff_hbm, cutoff), (relax_hbm, relax))
        )
    ]
    for copy in small:
        copy.start()
    tables[0].start()
    def load(f, _):
        pltpu.make_async_copy(field_hbm.at[f // levels, f % levels], field.at[f], field_sem.at[f]).start()
        return 0

    lax.fori_loop(0, F, load, 0)
    for copy in tables[1:]:
        copy.start()

    store[...] = jnp.zeros_like(store)
    for copy in small:
        copy.wait()
    for var in range(F // levels):
        store[var * levels : (var + 1) * levels, : 2 * NK * NK] = era[0, var]
    analysis = pack(analysis_rows(store[...]))
    me = gx * n_gy + gy
    mine = per_field([(owner[0, f // levels] == me).astype(jnp.int32) for f in range(F)])
    limit = per_field([cutoff[f // levels, f % levels] for f in range(F)])
    rate = per_field([relax[f // levels, f % levels] for f in range(F)])
    group, column = lanes_of((F, PACKED))
    start = jnp.full((F, PACKED), GROUP)
    for at, first in BACK_FROM.items():
        start = jnp.where(group == at, first, start)
    back = column >= start
    ky = jnp.where(back, group + FRONT, group + 1) // 2
    kx = jnp.where(back, GROUP - column, column + 1) // 2
    factor = jnp.where(ky * ky + kx * kx <= limit * limit, rate, 0.0)
    analysis = jnp.where(mine == 1, analysis, 0.0)

    tables[0].wait()

    def one(f, _):
        pltpu.make_async_copy(field_hbm.at[0, 0], field.at[f], field_sem.at[f]).wait()

        high, low = split(field[f])
        wide = dot(fy[...], high)
        band = wide[:SLOTS] + wide[32 : 32 + SLOTS] + dot(fy[:32], low)[:SLOTS]
        for tile in range(bands.shape[0]):
            bands[tile, pl.ds(f, SLOTS, stride=F), :] = band[:, 128 * tile : 128 * tile + 128]
        return 0

    lax.fori_loop(0, F, one, 0)
    tables[1].wait()
    high, low = split(jnp.concatenate([bands[tile] for tile in range(bands.shape[0])], axis=1))
    both = dot(high, fx[...]) + dot(low, fx[...])
    both = [both[:, 128 * way : 128 * way + 128] for way in range(2)]
    both = [way + pltpu.roll(way, 128 - GROUP, 1) for way in both]
    spectrum = pack([both[int(slot >= FRONT)][F * slot : F * slot + F] for slot in range(NK)])
    share[...] = factor * (analysis - spectrum)
    tables[2].wait()
    tables[3].wait()


def nudge_kernel(levels, chunk, mine, other, field, iy, ix, out_hbm, out, bands, sem):
    high, low = split(unpack(mine[...] + other[...]))
    wide = dot(high, ix[...]) + dot(low, ix[...])
    for tile in range(bands.shape[0]):
        bands[tile] = wide[:, 128 * tile : 128 * tile + 128]
    ny, nx = out.shape[1:]
    steps = ny // chunk

    def one(f, _):
        band = [bands[tile, pl.ds(f, SLOTS, stride=F), :] for tile in range(bands.shape[0])]
        band = jnp.concatenate(band, axis=1)
        high = band.astype(jnp.bfloat16).astype(jnp.float32)
        stacked = jnp.concatenate([high, high, band - high, jnp.zeros((128 - 3 * SLOTS, nx), jnp.float32)], axis=0)
        stacked = stacked.astype(jnp.bfloat16)
        for step in range(steps):
            at = pl.ds(step * chunk, chunk)
            out[f, at] = field[f, at] + dot(iy[at], stacked)
            pltpu.make_async_copy(
                out.at[f, at], out_hbm.at[f // levels, f % levels, at], sem.at[f * steps + step]
            ).start()
        return 0

    lax.fori_loop(0, F, one, 0)

    def end(n, _):
        f, step = n // steps, n % steps
        at = pl.ds(pl.multiple_of(step * chunk, chunk), chunk)
        pltpu.make_async_copy(out.at[f, at], out_hbm.at[f // levels, f % levels, at], sem.at[n]).wait()
        return 0

    lax.fori_loop(0, F * steps, end, 0)


def in_hbm(value):
    return pltpu.with_memory_space_constraint(jnp.asarray(value), pltpu.HBM)


def partners_of(n_gx, n_gy):
    core = n_gy
    along_x = [core | n_gy << bit for bit in range(1, n_gx.bit_length() - 1)]
    along_y = [core | 1 << bit for bit in range(n_gy.bit_length() - 1)]
    return [core] + along_x + along_y


def swap(value, size, bits):
    return lax.ppermute(value, ("gx", "gy"), [(i, i ^ bits) for i in range(size)])


def body(n_gx, n_gy, model_state, cutoff, relax_rate, owner_map, era_store):
    nvar, levels, ny, nx = model_state.shape
    fy, fx = forward_tables(n_gx, n_gy)
    iy, ix = inverse_tables(n_gx, n_gy)
    vmem = pl.BlockSpec(memory_space=pltpu.VMEM)
    hbm = pl.BlockSpec(memory_space=pltpu.HBM)
    share, field, iy, ix = pl.pallas_call(
        functools.partial(project_kernel, n_gy, levels),
        out_shape=(
            pltpu.VMEM((F, PACKED), jnp.float32),
            pltpu.VMEM((F, ny, nx), jnp.float32),
            pltpu.VMEM((ny, 128), jnp.bfloat16),
            pltpu.VMEM((256, nx), jnp.bfloat16),
        ),
        in_specs=[hbm] * 9,
        out_specs=[vmem] * 4,
        scratch_shapes=[
            pltpu.SMEM(owner_map.shape, jnp.int32),
            pltpu.SMEM(cutoff.shape, jnp.int32),
            pltpu.SMEM(relax_rate.shape, jnp.float32),
            pltpu.VMEM(era_store.shape, jnp.float32),
            pltpu.VMEM((F, 1024), jnp.float32),
            pltpu.VMEM((64, ny), jnp.bfloat16),
            pltpu.VMEM((nx, 256), jnp.bfloat16),
            pltpu.VMEM((nx // 128, SLOTS * F, 128), jnp.float32),
            pltpu.SemaphoreType.DMA((F,)),
            pltpu.SemaphoreType.DMA((4,)),
            pltpu.SemaphoreType.DMA((4,)),
        ],
        compiler_params=pltpu.CompilerParams(vmem_limit_bytes=20 * 2**20),
        name="project",
    )(*(in_hbm(value) for value in (owner_map, cutoff, relax_rate, era_store, model_state, fy, fx, iy, ix)))

    steps = partners_of(n_gx, n_gy)
    for bits in steps[:-1]:
        share = share + swap(share, n_gx * n_gy, bits)
    other = swap(share, n_gx * n_gy, steps[-1])

    chunk = min(ny, 256)
    nudged = pl.pallas_call(
        functools.partial(nudge_kernel, levels, chunk),
        out_shape=jax.ShapeDtypeStruct(model_state.shape, jnp.float32),
        in_specs=[vmem] * 5,
        out_specs=hbm,
        scratch_shapes=[
            pltpu.VMEM((F, ny, nx), jnp.float32),
            pltpu.VMEM((nx // 128, SLOTS * F, 128), jnp.float32),
            pltpu.SemaphoreType.DMA((F * (ny // chunk),)),
        ],
        compiler_params=pltpu.CompilerParams(vmem_limit_bytes=30 * 2**20),
        name="nudge",
    )(share, other, field, iy, ix)
    return nudged


def solution(mesh):
    n_gx, n_gy = mesh.shape["gx"], mesh.shape["gy"]
    placed = (
        P(None, "lev", "gy", "gx"),
        P(None, "lev"),
        P(None, "lev"),
        P("lev", None),
        P(("gx", "gy"), None, "lev", None),
    )
    return jax.shard_map(
        functools.partial(body, n_gx, n_gy),
        mesh=mesh,
        in_specs=placed,
        out_specs=P(None, "lev", "gy", "gx"),
        check_vma=False,
    )
```

```python
import functools

import jax
import jax.numpy as jnp
import ml_dtypes
import numpy as np
from jax import lax
from jax.experimental import pallas as pl
from jax.experimental.pallas import tpu as pltpu
from jax.sharding import PartitionSpec as P

NX = 2048
NY = 2048
KC = 10
NK = 21
F = 8
GROUP = 32
FRONT = 16
SLOTS = 24
PACKED = FRONT * GROUP
BACK_FROM = {1: 19, 2: 23, 3: 23, 4: 31, 5: 31}


def basis(positions, length):
    order = np.arange(NK)
    angle = np.mod(positions[:, None] * ((order + 1) // 2)[None, :], length) * (2 * np.pi / length)
    return np.where((order == 0) | (order % 2 == 1), np.cos(angle), np.sin(angle))


def halves(table):
    high = table.astype(ml_dtypes.bfloat16)
    low = (table - high.astype(np.float64)).astype(ml_dtypes.bfloat16)
    return high, low


def both_ways(high, low):
    table = np.zeros((high.shape[0], 8, GROUP), ml_dtypes.bfloat16)
    for group in range(4):
        half = low if group % 2 else high
        table[:, group, :NK] = half
        table[:, 4 + group, GROUP - NK :] = half[:, ::-1]
    return table.reshape(-1, 256)


def forward_tables(n_gx, n_gy):
    weight = np.where(np.arange(NK) == 0, 1.0, 2.0)
    high, low = halves(basis(np.arange(NY), NY) * weight / NY)
    ny = NY // n_gy
    along_y = np.zeros((n_gy, 64, ny), ml_dtypes.bfloat16)
    along_y[:, :NK] = high.reshape(n_gy, ny, NK).transpose(0, 2, 1)
    along_y[:, 32 : 32 + NK] = low.reshape(n_gy, ny, NK).transpose(0, 2, 1)
    high, low = halves(basis(np.arange(NX), NX) * weight / NX)
    nx = NX // n_gx
    along_x = both_ways(high, low).reshape(n_gx, nx, 256)
    return along_y, along_x


def inverse_tables(n_gx, n_gy):
    high, low = halves(basis(np.arange(NY), NY))
    ny = NY // n_gy
    along_y = np.zeros((n_gy, ny, 128), ml_dtypes.bfloat16)
    for first, half in ((0, high), (SLOTS, low), (2 * SLOTS, high)):
        along_y[:, :, first : first + NK] = half.reshape(n_gy, ny, NK)
    high, low = halves(basis(np.arange(NX), NX))
    nx = NX // n_gx
    along_x = both_ways(high, low).reshape(n_gx, nx, 256).transpose(0, 2, 1)
    return along_y, along_x


def split(value):
    high = value.astype(jnp.bfloat16)
    return high, (value - high.astype(jnp.float32)).astype(jnp.bfloat16)


def dot(left, right):
    return jnp.dot(left, right, preferred_element_type=jnp.float32)


def lanes_of(shape):
    lane = lax.broadcasted_iota(jnp.int32, shape, 1)
    return lane // GROUP, lane % GROUP


def analysis_rows(store):
    pieces = []
    for row in range(2 * NK):
        at = row * NK
        base = at // 128 * 128
        off = at - base
        width = 128 if off + NK <= 128 else 256
        window = store[:, base : base + width]
        pieces.append(pltpu.roll(window, (width - off) % width, 1)[:, :128] if off else window[:, :128])
    high, low = split(jnp.concatenate(pieces, axis=0))
    wave = lax.broadcasted_iota(jnp.int32, (128, 256), 0) - KC
    group, column = lanes_of((128, 256))
    column = jnp.where(group < 4, column, GROUP - 1 - column)
    number = (column + 1) // 2
    plus = jnp.where(wave == number, 1.0, 0.0)
    minus = jnp.where((wave == -number) & (number > 0), 1.0, 0.0)
    fold = jnp.where(column % 2 == 1, plus + minus, plus - minus)
    fold = jnp.where(column < NK, fold, 0.0).astype(jnp.bfloat16)
    folded = dot(high, fold) + dot(low, fold)
    column = lanes_of((8, 128))[1]
    rows = []
    for slot in range(NK):
        wave, back = (slot + 1) // 2, slot >= FRONT
        lanes = slice(128, 256) if back else slice(0, 128)
        along = GROUP - 1 - column if back else column
        even = (along == 0) | (along % 2 == 1)
        up, down = KC + wave, KC - wave
        real_up, real_down = (folded[8 * row : 8 * row + 8, lanes] for row in (up, down))
        imag_up, imag_down = (folded[8 * row : 8 * row + 8, lanes] for row in (NK + up, NK + down))
        if wave == 0:
            rows.append(jnp.where(even, real_up, -imag_up))
        elif slot % 2:
            rows.append(jnp.where(even, real_up + real_down, -(imag_up + imag_down)))
        else:
            rows.append(-jnp.where(even, imag_up - imag_down, real_up - real_down))
    return rows


def pack(rows):
    group, column = lanes_of((8, 128))
    blocks = []
    for block in range(FRONT // 4):
        total = jnp.zeros((8, 128), jnp.float32)
        for j in range(4):
            at = 4 * block + j
            total = jnp.where(group == j, rows[at], total)
            if at in BACK_FROM:
                total = jnp.where((group == j) & (column >= BACK_FROM[at]), rows[at + FRONT - 1], total)
        blocks.append(total)
    return jnp.concatenate(blocks, axis=1)


def unpack(packed):
    group, column = lanes_of((8, 128))
    zero = jnp.zeros((8, 128), jnp.float32)
    rows = [None] * SLOTS
    for block in range(FRONT // 4):
        here = packed[:, 128 * block : 128 * block + 128]
        after = pltpu.roll(here, GROUP, 1)
        for j in range(4):
            at = 4 * block + j
            row = jnp.where(group == j, here, jnp.where(group == (j + 1) % 4, after, 0.0))
            if at in BACK_FROM:
                back = column >= BACK_FROM[at]
                rows[at + FRONT - 1] = jnp.concatenate([zero, jnp.where(back, row, 0.0)], axis=1)
                row = jnp.where(back, 0.0, row)
            rows[at] = jnp.concatenate([row, zero], axis=1)
    empty = jnp.zeros((8, 256), jnp.float32)
    return jnp.concatenate([empty if row is None else row for row in rows], axis=0)


def per_field(values):
    row = lax.broadcasted_iota(jnp.int32, (F, 1), 0)
    total = jnp.full((F, 1), values[0])
    for field in range(1, F):
        total = jnp.where(row == field, values[field], total)
    return total


def project_kernel(
    n_gy, levels, owner_hbm, cutoff_hbm, relax_hbm, era_hbm, field_hbm, fy_hbm, fx_hbm, iy_hbm, ix_hbm,
    share, field, iy, ix, owner, cutoff, relax, era, store, fy, fx, bands, field_sem, small_sem, table_sem,
):
    gx, gy = lax.axis_index("gx"), lax.axis_index("gy")
    tables = [
        pltpu.make_async_copy(src, dst, table_sem.at[n])
        for n, (src, dst) in enumerate(
            ((fy_hbm.at[gy], fy), (fx_hbm.at[gx], fx), (iy_hbm.at[gy], iy), (ix_hbm.at[gx], ix))
        )
    ]
    small = [
        pltpu.make_async_copy(src, dst, small_sem.at[n])
        for n, (src, dst) in enumerate(
            ((era_hbm, era), (owner_hbm, owner), (cutoff_hbm, cutoff), (relax_hbm, relax))
        )
    ]
    for copy in small:
        copy.start()
    tables[0].start()
    def load(f, _):
        pltpu.make_async_copy(field_hbm.at[f // levels, f % levels], field.at[f], field_sem.at[f]).start()
        return 0

    lax.fori_loop(0, F, load, 0)
    for copy in tables[1:]:
        copy.start()

    store[...] = jnp.zeros_like(store)
    for copy in small:
        copy.wait()
    for var in range(F // levels):
        store[var * levels : (var + 1) * levels, : 2 * NK * NK] = era[0, var]
    analysis = pack(analysis_rows(store[...]))
    me = gx * n_gy + gy
    mine = per_field([(owner[0, f // levels] == me).astype(jnp.int32) for f in range(F)])
    limit = per_field([cutoff[f // levels, f % levels] for f in range(F)])
    rate = per_field([relax[f // levels, f % levels] for f in range(F)])
    group, column = lanes_of((F, PACKED))
    start = jnp.full((F, PACKED), GROUP)
    for at, first in BACK_FROM.items():
        start = jnp.where(group == at, first, start)
    back = column >= start
    ky = jnp.where(back, group + FRONT, group + 1) // 2
    kx = jnp.where(back, GROUP - column, column + 1) // 2
    factor = jnp.where(ky * ky + kx * kx <= limit * limit, rate, 0.0)
    analysis = jnp.where(mine == 1, analysis, 0.0)

    tables[0].wait()

    def one(f, _):
        pltpu.make_async_copy(field_hbm.at[0, 0], field.at[f], field_sem.at[f]).wait()

        high, low = split(field[f])
        wide = dot(fy[...], high)
        band = wide[:SLOTS] + wide[32 : 32 + SLOTS] + dot(fy[:32], low)[:SLOTS]
        for tile in range(bands.shape[0]):
            bands[tile, pl.ds(f, SLOTS, stride=F), :] = band[:, 128 * tile : 128 * tile + 128]
        return 0

    lax.fori_loop(0, F, one, 0)
    tables[1].wait()
    high, low = split(jnp.concatenate([bands[tile] for tile in range(bands.shape[0])], axis=1))
    both = dot(high, fx[...]) + dot(low, fx[...])
    both = [both[:, 128 * way : 128 * way + 128] for way in range(2)]
    both = [way + pltpu.roll(way, 128 - GROUP, 1) for way in both]
    spectrum = pack([both[int(slot >= FRONT)][F * slot : F * slot + F] for slot in range(NK)])
    share[...] = factor * (analysis - spectrum)
    tables[2].wait()
    tables[3].wait()


def nudge_kernel(levels, chunk, mine, other, field, iy, ix, out_hbm, out, bands, sem):
    rows = unpack(mine[...] + other[...])
    for tile in range(2):
        bands[tile] = rows[:, 128 * tile : 128 * tile + 128]
    ny, nx = out.shape[1:]
    steps = ny // chunk

    def one(f, _):
        rows = [bands[tile, pl.ds(f, SLOTS, stride=F), :] for tile in range(2)]
        rows = jnp.concatenate(rows, axis=1)
        high = rows.astype(jnp.bfloat16).astype(jnp.float32)
        pad = jnp.zeros((8, 256), jnp.float32)
        rows = jnp.concatenate([high, pad, rows - high, pad], axis=0).astype(jnp.bfloat16)
        wide = dot(rows, ix[...])
        band = wide[:SLOTS] + wide[32 : 32 + SLOTS]
        high = band.astype(jnp.bfloat16).astype(jnp.float32)
        stacked = jnp.concatenate([high, high, band - high, jnp.zeros((128 - 3 * SLOTS, nx), jnp.float32)], axis=0)
        stacked = stacked.astype(jnp.bfloat16)
        for step in range(steps):
            at = pl.ds(step * chunk, chunk)
            out[f, at] = field[f, at] + dot(iy[at], stacked)
            pltpu.make_async_copy(
                out.at[f, at], out_hbm.at[f // levels, f % levels, at], sem.at[f * steps + step]
            ).start()
        return 0

    lax.fori_loop(0, F, one, 0, unroll=8)

    def end(n, _):
        f, step = n // steps, n % steps
        at = pl.ds(pl.multiple_of(step * chunk, chunk), chunk)
        pltpu.make_async_copy(out.at[f, at], out_hbm.at[f // levels, f % levels, at], sem.at[n]).wait()
        return 0

    lax.fori_loop(0, F * steps, end, 0)


def in_hbm(value):
    return pltpu.with_memory_space_constraint(jnp.asarray(value), pltpu.HBM)


def partners_of(n_gx, n_gy):
    core = n_gy
    along_x = [core | n_gy << bit for bit in range(1, n_gx.bit_length() - 1)]
    along_y = [core | 1 << bit for bit in range(n_gy.bit_length() - 1)]
    return [core] + along_x + along_y


def swap(value, size, bits):
    return lax.ppermute(value, ("gx", "gy"), [(i, i ^ bits) for i in range(size)])


def body(n_gx, n_gy, model_state, cutoff, relax_rate, owner_map, era_store):
    nvar, levels, ny, nx = model_state.shape
    fy, fx = forward_tables(n_gx, n_gy)
    iy, ix = inverse_tables(n_gx, n_gy)
    vmem = pl.BlockSpec(memory_space=pltpu.VMEM)
    hbm = pl.BlockSpec(memory_space=pltpu.HBM)
    share, field, iy, ix = pl.pallas_call(
        functools.partial(project_kernel, n_gy, levels),
        out_shape=(
            pltpu.VMEM((F, PACKED), jnp.float32),
            pltpu.VMEM((F, ny, nx), jnp.float32),
            pltpu.VMEM((ny, 128), jnp.bfloat16),
            pltpu.VMEM((256, nx), jnp.bfloat16),
        ),
        in_specs=[hbm] * 9,
        out_specs=[vmem] * 4,
        scratch_shapes=[
            pltpu.SMEM(owner_map.shape, jnp.int32),
            pltpu.SMEM(cutoff.shape, jnp.int32),
            pltpu.SMEM(relax_rate.shape, jnp.float32),
            pltpu.VMEM(era_store.shape, jnp.float32),
            pltpu.VMEM((F, 1024), jnp.float32),
            pltpu.VMEM((64, ny), jnp.bfloat16),
            pltpu.VMEM((nx, 256), jnp.bfloat16),
            pltpu.VMEM((nx // 128, SLOTS * F, 128), jnp.float32),
            pltpu.SemaphoreType.DMA((F,)),
            pltpu.SemaphoreType.DMA((4,)),
            pltpu.SemaphoreType.DMA((4,)),
        ],
        compiler_params=pltpu.CompilerParams(vmem_limit_bytes=20 * 2**20),
        name="project",
    )(*(in_hbm(value) for value in (owner_map, cutoff, relax_rate, era_store, model_state, fy, fx, iy, ix)))

    steps = partners_of(n_gx, n_gy)
    for bits in steps[:-1]:
        share = share + swap(share, n_gx * n_gy, bits)
    other = swap(share, n_gx * n_gy, steps[-1])

    chunk = min(ny, 256)
    nudged = pl.pallas_call(
        functools.partial(nudge_kernel, levels, chunk),
        out_shape=jax.ShapeDtypeStruct(model_state.shape, jnp.float32),
        in_specs=[vmem] * 5,
        out_specs=hbm,
        scratch_shapes=[
            pltpu.VMEM((F, ny, nx), jnp.float32),
            pltpu.VMEM((2, SLOTS * F, 128), jnp.float32),
            pltpu.SemaphoreType.DMA((F * (ny // chunk),)),
        ],
        compiler_params=pltpu.CompilerParams(vmem_limit_bytes=30 * 2**20),
        name="nudge",
    )(share, other, field, iy, ix)
    return nudged


def solution(mesh):
    n_gx, n_gy = mesh.shape["gx"], mesh.shape["gy"]
    placed = (
        P(None, "lev", "gy", "gx"),
        P(None, "lev"),
        P(None, "lev"),
        P("lev", None),
        P(("gx", "gy"), None, "lev", None),
    )
    return jax.shard_map(
        functools.partial(body, n_gx, n_gy),
        mesh=mesh,
        in_specs=placed,
        out_specs=P(None, "lev", "gy", "gx"),
        check_vma=False,
    )
```

```python
import functools

import jax
import jax.numpy as jnp
import ml_dtypes
import numpy as np
from jax import lax
from jax.experimental import pallas as pl
from jax.experimental.pallas import tpu as pltpu
from jax.sharding import PartitionSpec as P

NX = 2048
NY = 2048
KC = 10
NK = 21
F = 8
GROUP = 32
FRONT = 16
SLOTS = 24
PACKED = FRONT * GROUP
BACK_FROM = {1: 19, 2: 23, 3: 23, 4: 31, 5: 31}


def basis(positions, length):
    order = np.arange(NK)
    angle = np.mod(positions[:, None] * ((order + 1) // 2)[None, :], length) * (2 * np.pi / length)
    return np.where((order == 0) | (order % 2 == 1), np.cos(angle), np.sin(angle))


def halves(table):
    high = table.astype(ml_dtypes.bfloat16)
    low = (table - high.astype(np.float64)).astype(ml_dtypes.bfloat16)
    return high, low


def both_ways(high, low):
    table = np.zeros((high.shape[0], 8, GROUP), ml_dtypes.bfloat16)
    for group in range(4):
        half = low if group % 2 else high
        table[:, group, :NK] = half
        table[:, 4 + group, GROUP - NK :] = half[:, ::-1]
    return table.reshape(-1, 256)


def forward_tables(n_gx, n_gy):
    weight = np.where(np.arange(NK) == 0, 1.0, 2.0)
    high, low = halves(basis(np.arange(NY), NY) * weight / NY)
    ny = NY // n_gy
    along_y = np.zeros((n_gy, 64, ny), ml_dtypes.bfloat16)
    along_y[:, :NK] = high.reshape(n_gy, ny, NK).transpose(0, 2, 1)
    along_y[:, 32 : 32 + NK] = low.reshape(n_gy, ny, NK).transpose(0, 2, 1)
    high, low = halves(basis(np.arange(NX), NX) * weight / NX)
    nx = NX // n_gx
    along_x = both_ways(high, low).reshape(n_gx, nx, 256)
    return along_y, along_x


def inverse_tables(n_gx, n_gy):
    high, low = halves(basis(np.arange(NY), NY))
    ny = NY // n_gy
    along_y = np.zeros((n_gy, ny, 128), ml_dtypes.bfloat16)
    for first, half in ((0, high), (SLOTS, low), (2 * SLOTS, high)):
        along_y[:, :, first : first + NK] = half.reshape(n_gy, ny, NK)
    high, low = halves(basis(np.arange(NX), NX))
    nx = NX // n_gx
    along_x = both_ways(high, low).reshape(n_gx, nx, 256).transpose(0, 2, 1)
    return along_y, along_x


def split(value):
    high = value.astype(jnp.bfloat16)
    return high, (value - high.astype(jnp.float32)).astype(jnp.bfloat16)


def dot(left, right):
    return jnp.dot(left, right, preferred_element_type=jnp.float32)


def lanes_of(shape):
    lane = lax.broadcasted_iota(jnp.int32, shape, 1)
    return lane // GROUP, lane % GROUP


def analysis_rows(store):
    pieces = []
    for row in range(2 * NK):
        at = row * NK
        base = at // 128 * 128
        off = at - base
        width = 128 if off + NK <= 128 else 256
        window = store[:, base : base + width]
        pieces.append(pltpu.roll(window, (width - off) % width, 1)[:, :128] if off else window[:, :128])
    high, low = split(jnp.concatenate(pieces, axis=0))
    wave = lax.broadcasted_iota(jnp.int32, (128, 256), 0) - KC
    group, column = lanes_of((128, 256))
    column = jnp.where(group < 4, column, GROUP - 1 - column)
    number = (column + 1) // 2
    plus = jnp.where(wave == number, 1.0, 0.0)
    minus = jnp.where((wave == -number) & (number > 0), 1.0, 0.0)
    fold = jnp.where(column % 2 == 1, plus + minus, plus - minus)
    fold = jnp.where(column < NK, fold, 0.0).astype(jnp.bfloat16)
    folded = dot(high, fold) + dot(low, fold)
    column = lanes_of((8, 128))[1]
    rows = []
    for slot in range(NK):
        wave, back = (slot + 1) // 2, slot >= FRONT
        lanes = slice(128, 256) if back else slice(0, 128)
        along = GROUP - 1 - column if back else column
        even = (along == 0) | (along % 2 == 1)
        up, down = KC + wave, KC - wave
        real_up, real_down = (folded[8 * row : 8 * row + 8, lanes] for row in (up, down))
        imag_up, imag_down = (folded[8 * row : 8 * row + 8, lanes] for row in (NK + up, NK + down))
        if wave == 0:
            rows.append(jnp.where(even, real_up, -imag_up))
        elif slot % 2:
            rows.append(jnp.where(even, real_up + real_down, -(imag_up + imag_down)))
        else:
            rows.append(-jnp.where(even, imag_up - imag_down, real_up - real_down))
    return rows


def pack(rows):
    group, column = lanes_of((8, 128))
    blocks = []
    for block in range(FRONT // 4):
        total = jnp.zeros((8, 128), jnp.float32)
        for j in range(4):
            at = 4 * block + j
            total = jnp.where(group == j, rows[at], total)
            if at in BACK_FROM:
                total = jnp.where((group == j) & (column >= BACK_FROM[at]), rows[at + FRONT - 1], total)
        blocks.append(total)
    return jnp.concatenate(blocks, axis=1)


def unpack(packed):
    group, column = lanes_of((8, 128))
    zero = jnp.zeros((8, 128), jnp.float32)
    rows = [None] * SLOTS
    for block in range(FRONT // 4):
        here = packed[:, 128 * block : 128 * block + 128]
        after = pltpu.roll(here, GROUP, 1)
        for j in range(4):
            at = 4 * block + j
            row = jnp.where(group == j, here, jnp.where(group == (j + 1) % 4, after, 0.0))
            if at in BACK_FROM:
                back = column >= BACK_FROM[at]
                rows[at + FRONT - 1] = jnp.concatenate([zero, jnp.where(back, row, 0.0)], axis=1)
                row = jnp.where(back, 0.0, row)
            rows[at] = jnp.concatenate([row, zero], axis=1)
    empty = jnp.zeros((8, 256), jnp.float32)
    return jnp.concatenate([empty if row is None else row for row in rows], axis=0)


def per_field(values):
    row = lax.broadcasted_iota(jnp.int32, (F, 1), 0)
    total = jnp.full((F, 1), values[0])
    for field in range(1, F):
        total = jnp.where(row == field, values[field], total)
    return total


def project_kernel(
    n_gy, levels, owner_hbm, cutoff_hbm, relax_hbm, era_hbm, field_hbm, fy_hbm, fx_hbm, iy_hbm, ix_hbm,
    share, field, iy, ix, owner, cutoff, relax, era, store, fy, fx, bands, field_sem, small_sem, table_sem,
):
    gx, gy = lax.axis_index("gx"), lax.axis_index("gy")
    tables = [
        pltpu.make_async_copy(src, dst, table_sem.at[n])
        for n, (src, dst) in enumerate(
            ((fy_hbm.at[gy], fy), (fx_hbm.at[gx], fx), (iy_hbm.at[gy], iy), (ix_hbm.at[gx], ix))
        )
    ]
    small = [
        pltpu.make_async_copy(src, dst, small_sem.at[n])
        for n, (src, dst) in enumerate(
            ((era_hbm, era), (owner_hbm, owner), (cutoff_hbm, cutoff), (relax_hbm, relax))
        )
    ]
    for copy in small:
        copy.start()
    tables[0].start()
    def load(f, _):
        pltpu.make_async_copy(field_hbm.at[f // levels, f % levels], field.at[f], field_sem.at[f]).start()
        return 0

    lax.fori_loop(0, F, load, 0)
    for copy in tables[1:]:
        copy.start()

    store[...] = jnp.zeros_like(store)
    for copy in small:
        copy.wait()
    for var in range(F // levels):
        store[var * levels : (var + 1) * levels, : 2 * NK * NK] = era[0, var]
    analysis = pack(analysis_rows(store[...]))
    me = gx * n_gy + gy
    mine = per_field([(owner[0, f // levels] == me).astype(jnp.int32) for f in range(F)])
    limit = per_field([cutoff[f // levels, f % levels] for f in range(F)])
    rate = per_field([relax[f // levels, f % levels] for f in range(F)])
    group, column = lanes_of((F, PACKED))
    start = jnp.full((F, PACKED), GROUP)
    for at, first in BACK_FROM.items():
        start = jnp.where(group == at, first, start)
    back = column >= start
    ky = jnp.where(back, group + FRONT, group + 1) // 2
    kx = jnp.where(back, GROUP - column, column + 1) // 2
    factor = jnp.where(ky * ky + kx * kx <= limit * limit, rate, 0.0)
    analysis = jnp.where(mine == 1, analysis, 0.0)

    tables[0].wait()

    def one(f, _):
        pltpu.make_async_copy(field_hbm.at[0, 0], field.at[f], field_sem.at[f]).wait()

        high, low = split(field[f])
        wide = dot(fy[...], high)
        band = wide[:SLOTS] + wide[32 : 32 + SLOTS] + dot(fy[:32], low)[:SLOTS]
        for tile in range(bands.shape[0]):
            bands[tile, pl.ds(f, SLOTS, stride=F), :] = band[:, 128 * tile : 128 * tile + 128]
        return 0

    lax.fori_loop(0, F, one, 0, unroll=2)
    tables[1].wait()
    high, low = split(jnp.concatenate([bands[tile] for tile in range(bands.shape[0])], axis=1))
    both = dot(high, fx[...]) + dot(low, fx[...])
    both = [both[:, 128 * way : 128 * way + 128] for way in range(2)]
    both = [way + pltpu.roll(way, 128 - GROUP, 1) for way in both]
    spectrum = pack([both[int(slot >= FRONT)][F * slot : F * slot + F] for slot in range(NK)])
    share[...] = factor * (analysis - spectrum)
    tables[2].wait()
    tables[3].wait()


def nudge_kernel(levels, chunk, mine, other, field, iy, ix, out_hbm, out, bands, sem):
    rows = unpack(mine[...] + other[...])
    for tile in range(2):
        bands[tile] = rows[:, 128 * tile : 128 * tile + 128]
    ny, nx = out.shape[1:]
    steps = ny // chunk

    def one(f, _):
        rows = [bands[tile, pl.ds(f, SLOTS, stride=F), :] for tile in range(2)]
        rows = jnp.concatenate(rows, axis=1)
        high = rows.astype(jnp.bfloat16).astype(jnp.float32)
        pad = jnp.zeros((8, 256), jnp.float32)
        rows = jnp.concatenate([high, pad, rows - high, pad], axis=0).astype(jnp.bfloat16)
        wide = dot(rows, ix[...])
        band = wide[:SLOTS] + wide[32 : 32 + SLOTS]
        high = band.astype(jnp.bfloat16).astype(jnp.float32)
        stacked = jnp.concatenate([high, high, band - high, jnp.zeros((128 - 3 * SLOTS, nx), jnp.float32)], axis=0)
        stacked = stacked.astype(jnp.bfloat16)
        for step in range(steps):
            at = pl.ds(step * chunk, chunk)
            out[f, at] = field[f, at] + dot(iy[at], stacked)
            pltpu.make_async_copy(
                out.at[f, at], out_hbm.at[f // levels, f % levels, at], sem.at[f * steps + step]
            ).start()
        return 0

    lax.fori_loop(0, F, one, 0, unroll=8)

    def end(n, _):
        f, step = n // steps, n % steps
        at = pl.ds(pl.multiple_of(step * chunk, chunk), chunk)
        pltpu.make_async_copy(out.at[f, at], out_hbm.at[f // levels, f % levels, at], sem.at[n]).wait()
        return 0

    lax.fori_loop(0, F * steps, end, 0)


def in_hbm(value):
    return pltpu.with_memory_space_constraint(jnp.asarray(value), pltpu.HBM)


def partners_of(n_gx, n_gy):
    core = n_gy
    along_x = [core | n_gy << bit for bit in range(1, n_gx.bit_length() - 1)]
    along_y = [core | 1 << bit for bit in range(n_gy.bit_length() - 1)]
    return [core] + along_x + along_y


def swap(value, size, bits):
    return lax.ppermute(value, ("gx", "gy"), [(i, i ^ bits) for i in range(size)])


def body(n_gx, n_gy, model_state, cutoff, relax_rate, owner_map, era_store):
    nvar, levels, ny, nx = model_state.shape
    fy, fx = forward_tables(n_gx, n_gy)
    iy, ix = inverse_tables(n_gx, n_gy)
    vmem = pl.BlockSpec(memory_space=pltpu.VMEM)
    hbm = pl.BlockSpec(memory_space=pltpu.HBM)
    share, field, iy, ix = pl.pallas_call(
        functools.partial(project_kernel, n_gy, levels),
        out_shape=(
            pltpu.VMEM((F, PACKED), jnp.float32),
            pltpu.VMEM((F, ny, nx), jnp.float32),
            pltpu.VMEM((ny, 128), jnp.bfloat16),
            pltpu.VMEM((256, nx), jnp.bfloat16),
        ),
        in_specs=[hbm] * 9,
        out_specs=[vmem] * 4,
        scratch_shapes=[
            pltpu.SMEM(owner_map.shape, jnp.int32),
            pltpu.SMEM(cutoff.shape, jnp.int32),
            pltpu.SMEM(relax_rate.shape, jnp.float32),
            pltpu.VMEM(era_store.shape, jnp.float32),
            pltpu.VMEM((F, 1024), jnp.float32),
            pltpu.VMEM((64, ny), jnp.bfloat16),
            pltpu.VMEM((nx, 256), jnp.bfloat16),
            pltpu.VMEM((nx // 128, SLOTS * F, 128), jnp.float32),
            pltpu.SemaphoreType.DMA((F,)),
            pltpu.SemaphoreType.DMA((4,)),
            pltpu.SemaphoreType.DMA((4,)),
        ],
        compiler_params=pltpu.CompilerParams(vmem_limit_bytes=20 * 2**20),
        name="project",
    )(*(in_hbm(value) for value in (owner_map, cutoff, relax_rate, era_store, model_state, fy, fx, iy, ix)))

    steps = partners_of(n_gx, n_gy)
    for bits in steps[:-1]:
        share = share + swap(share, n_gx * n_gy, bits)
    other = swap(share, n_gx * n_gy, steps[-1])

    chunk = min(ny, 256)
    nudged = pl.pallas_call(
        functools.partial(nudge_kernel, levels, chunk),
        out_shape=jax.ShapeDtypeStruct(model_state.shape, jnp.float32),
        in_specs=[vmem] * 5,
        out_specs=hbm,
        scratch_shapes=[
            pltpu.VMEM((F, ny, nx), jnp.float32),
            pltpu.VMEM((2, SLOTS * F, 128), jnp.float32),
            pltpu.SemaphoreType.DMA((F * (ny // chunk),)),
        ],
        compiler_params=pltpu.CompilerParams(vmem_limit_bytes=30 * 2**20),
        name="nudge",
    )(share, other, field, iy, ix)
    return nudged


def solution(mesh):
    n_gx, n_gy = mesh.shape["gx"], mesh.shape["gy"]
    placed = (
        P(None, "lev", "gy", "gx"),
        P(None, "lev"),
        P(None, "lev"),
        P("lev", None),
        P(("gx", "gy"), None, "lev", None),
    )
    return jax.shard_map(
        functools.partial(body, n_gx, n_gy),
        mesh=mesh,
        in_specs=placed,
        out_specs=P(None, "lev", "gy", "gx"),
        check_vma=False,
    )
```
